512 devices in a mesh: rows: 16 (over z, core), cols: 32 (over y, x).
Axes of the slice: x: 4, y: 8, z: 8, core: 2. Of those that a mesh axis runs over, the one named last changes fastest.
Arguments:
- query_feats: bfloat16 [256, 256, 512], P('rows', 'cols'), may hold values from -6 to 6
- key_feats: bfloat16 [256, 256, 512], P('rows', 'cols'), may hold values from -6 to 6
- value_feats: bfloat16 [256, 256, 512], P('rows', 'cols'), may hold values from -6 to 6
- proj_weight: bfloat16 [8, 64, 256], replicated, may hold values from -3 to 3
- cotangent: bfloat16 [256, 256, 512], P('rows', 'cols'), may hold values from -6 to 6
Outputs:
- attended: bfloat16 [256, 256, 512], P('rows', 'cols')
- grad_query: bfloat16 [256, 256, 512], P('rows', 'cols')
- grad_key: bfloat16 [256, 256, 512], P('rows', 'cols')
- grad_value: bfloat16 [256, 256, 512], P('rows', 'cols')
- grad_proj: float32 [8, 64, 256], replicated
The draws below stay inside these ranges and needn't reach their ends.
All inputs are finite; a program needn't handle non-finite values.
Results may differ from the reference program's by a relative error of at most 0.012.
The reference program's roundings to bfloat16 on the way count: a program that leaves them out, or rounds other values in their place, can miss the bound.
Values may be sent and summed in bfloat16 or wider, within the bound.
No kernel may reach another device: no remote copies, remote signals or barrier semaphores. Data moves between devices by JAX's collectives and lax.ppermute only.
A program may use at most 128 MiB of HBM per device.

```python
import jax
import jax.numpy as jnp
from jax import lax

HEADS = 8
HD = 64
LAND = 256
RAD = 8
TILE_ROWS = 8
CC = 8
FEAT = 512
NR = 256
NC = 256


def rough_field(key):
    normal = jnp.clip(jax.random.normal(jax.random.fold_in(key, 11), (NR, NC, HEADS * HD), jnp.float32), -4.0, 4.0)
    return normal


def draw_query_feats(key, part):
    field = rough_field(jax.random.fold_in(key, 21))
    return field.astype(jnp.bfloat16)


def draw_key_feats(key, part):
    field = rough_field(jax.random.fold_in(key, 22))
    return field.astype(jnp.bfloat16)


def draw_proj_weight(key, part):
    return jnp.clip(0.75 * jax.random.normal(jax.random.fold_in(key, 32), (HEADS, HD, LAND), jnp.float32), -3.0, 3.0).astype(jnp.bfloat16)


def block_levels(own_key, extent, cuts, least, top_value):
    def one(axis_at, parts):
        steps = jax.random.uniform(jax.random.fold_in(jax.random.fold_in(own_key, 6), axis_at), (parts,), jnp.float32, least / len(cuts), top_value / len(cuts))
        return jnp.repeat(jnp.exp(steps), extent[axis_at] // parts).reshape((-1,) + (1,) * (len(extent) - axis_at - 1))

    level = one(*cuts[0])
    for cut in cuts[1:]:
        level = level * one(*cut)
    return level


def scatter_about(rng, shape, scale, reach, split=(), kind=jnp.bfloat16):
    values = jax.random.normal(rng, shape, jnp.float32) * scale
    if len(split) > 0:
        values = block_levels(rng, shape, split, -0.22, 0.18) * values
    return jnp.clip(values, min=-reach, max=reach).astype(kind)


def setup_inputs(seed: int = 0) -> dict:
    keys = jax.random.split(jax.random.key(seed), 6)
    query_feats = draw_query_feats(jax.random.fold_in(keys[5], 71), 0)
    key_feats = draw_key_feats(jax.random.fold_in(keys[5], 71), 0)
    value_feats = scatter_about(keys[2], (NR, NC, FEAT), 1.0, 6.0, ((0, 16), (1, 32)))
    proj_weight = draw_proj_weight(jax.random.fold_in(keys[5], 71), 0)
    cotangent = scatter_about(keys[4], (NR, NC, FEAT), 1.0, 6.0, ((0, 16), (1, 32)))
    return {"query_feats": query_feats, "key_feats": key_feats, "value_feats": value_feats, "proj_weight": proj_weight, "cotangent": cotangent}


HIGH_PREC = lax.Precision.HIGHEST


def window_mask(band_rows, band_cols, radius):
    query_row = jnp.arange(band_rows)[:, None, None, None]
    query_col = jnp.arange(band_cols)[None, :, None, None]
    key_row = jnp.arange(band_rows + 2 * radius)[None, None, :, None]
    key_col = jnp.arange(band_cols + 2 * radius)[None, None, None, :]
    inside = (jnp.abs(key_row - radius - query_row) <= radius) & (jnp.abs(key_col - radius - query_col) <= radius)
    return inside.reshape(band_rows * band_cols, (band_rows + 2 * radius) * (band_cols + 2 * radius))


def as_float(array):
    return array.astype(jnp.float32)


def attend_tile(query_tile, key_region, value_region, allowed, key_marks, value_marks, score_scale):
    score_win = jnp.einsum("qhd,khd->hqk", as_float(query_tile), as_float(key_region)) * score_scale
    score_win = jnp.where(allowed[None], score_win, -jnp.inf)
    score_mark = jnp.einsum("qhd,hld->hql", as_float(query_tile), as_float(key_marks)) * score_scale
    row_top = jnp.maximum(jnp.max(score_win, -1), jnp.max(score_mark, -1))
    row_total = jnp.sum(jnp.exp(score_win - row_top[..., None]), -1) + jnp.sum(jnp.exp(score_mark - row_top[..., None]), -1)
    log_total = row_top + jnp.log(row_total)
    weight_win = jnp.exp(score_win - log_total[..., None]).astype(jnp.bfloat16)
    weight_mark = jnp.exp(score_mark - log_total[..., None]).astype(jnp.bfloat16)
    mixed_out = jnp.einsum("hqk,khd->qhd", as_float(weight_win), as_float(value_region))
    mixed_out = mixed_out + jnp.einsum("hql,hld->qhd", as_float(weight_mark), as_float(value_marks))
    return mixed_out, log_total


def query_grads(query_tile, grad_tile, key_region, value_region, allowed, key_marks, value_marks, log_total, delta_term, score_scale):
    score_win = jnp.einsum("qhd,khd->hqk", as_float(query_tile), as_float(key_region)) * score_scale
    score_win = jnp.where(allowed[None], score_win, -jnp.inf)
    score_mark = jnp.einsum("qhd,hld->hql", as_float(query_tile), as_float(key_marks)) * score_scale
    prob_win = jnp.exp(score_win - log_total[..., None])
    prob_mark = jnp.exp(score_mark - log_total[..., None])
    inner_win = jnp.einsum("qhd,khd->hqk", as_float(grad_tile), as_float(value_region))
    inner_mark = jnp.einsum("qhd,hld->hql", as_float(grad_tile), as_float(value_marks))
    dscore_win = (prob_win * (inner_win - delta_term[..., None])).astype(jnp.bfloat16)
    dscore_mark = (prob_mark * (inner_mark - delta_term[..., None])).astype(jnp.bfloat16)
    grad_q = jnp.einsum("hqk,khd->qhd", as_float(dscore_win), as_float(key_region))
    grad_q = (grad_q + jnp.einsum("hql,hld->qhd", as_float(dscore_mark), as_float(key_marks))) * score_scale
    key_part = jnp.einsum("hql,qhd->hld", as_float(dscore_mark), as_float(query_tile)) * score_scale
    value_part = jnp.einsum("hql,qhd->hld", as_float(prob_mark.astype(jnp.bfloat16)), as_float(grad_tile))
    return grad_q, key_part, value_part


def key_grads(key_tile, value_tile, query_region, grad_region, allowed, log_region, delta_region, score_scale):
    score_key = jnp.einsum("khd,qhd->hkq", as_float(key_tile), as_float(query_region)) * score_scale
    score_key = jnp.where(allowed[None], score_key, -jnp.inf)
    prob_key = jnp.exp(score_key - log_region[:, None, :])
    inner_key = jnp.einsum("khd,qhd->hkq", as_float(value_tile), as_float(grad_region))
    dscore_key = (prob_key * (inner_key - delta_region[:, None, :])).astype(jnp.bfloat16)
    grad_k = jnp.einsum("hkq,qhd->khd", as_float(dscore_key), as_float(query_region)) * score_scale
    grad_v = jnp.einsum("hkq,qhd->khd", as_float(prob_key.astype(jnp.bfloat16)), as_float(grad_region))
    return grad_k, grad_v


def reference(query_feats, key_feats, value_feats, proj_weight, cotangent):
    grid_rows, grid_cols, feature_count = query_feats.shape
    head_count, head_dim, mark_count = proj_weight.shape
    score_scale = head_dim ** -0.5
    token_count = grid_rows * grid_cols
    key_heads = key_feats.reshape(token_count, head_count, head_dim).transpose(1, 0, 2)
    value_heads = value_feats.reshape(token_count, head_count, head_dim).transpose(1, 0, 2)

    def landmark_means(operands):
        key_head, value_head, weight_head = operands
        logits = jnp.dot(key_head, weight_head, preferred_element_type=jnp.float32)
        exp_terms = jnp.exp(logits - jnp.max(logits, 0))
        column_total = jnp.sum(exp_terms, 0)
        key_mean = jnp.dot(exp_terms.T, as_float(key_head), precision=HIGH_PREC) / column_total[:, None]
        value_mean = jnp.dot(exp_terms.T, as_float(value_head), precision=HIGH_PREC) / column_total[:, None]
        return key_mean, value_mean

    key_mean, value_mean = lax.map(landmark_means, (key_heads, value_heads, proj_weight))
    key_marks = key_mean.astype(jnp.bfloat16)
    value_marks = value_mean.astype(jnp.bfloat16)

    band_count = grid_rows // TILE_ROWS
    strip_count = grid_cols // CC
    tile_count = band_count * strip_count
    region_rows = TILE_ROWS + 2 * RAD
    region_cols = CC + 2 * RAD
    window_near = window_mask(TILE_ROWS, CC, RAD)
    pad_spec = ((RAD, RAD), (RAD, RAD), (0, 0))
    padded_kv = jnp.pad(jnp.concatenate([key_feats, value_feats], -1), pad_spec)
    tile_ids = jnp.arange(tile_count, dtype=jnp.int32)

    def tile_anchor(tile_index):
        return (tile_index // strip_count) * TILE_ROWS, (tile_index % strip_count) * CC

    def allowed_at(row_first, col_first):
        region_row = row_first - RAD + jnp.arange(region_rows, dtype=jnp.int32)
        region_col = col_first - RAD + jnp.arange(region_cols, dtype=jnp.int32)
        inside = ((region_row >= 0) & (region_row < grid_rows))[:, None] & ((region_col >= 0) & (region_col < grid_cols))[None, :]
        return window_near & inside.reshape(-1)[None, :]

    def take_block(source, row_first, col_first, height, breadth):
        return lax.dynamic_slice(source, (row_first, col_first, jnp.int32(0)), (height, breadth, source.shape[2]))

    def to_grid(tile_stack, breadth):
        shaped = tile_stack.reshape(band_count, strip_count, TILE_ROWS, CC, breadth)
        return shaped.transpose(0, 2, 1, 3, 4).reshape(grid_rows, grid_cols, breadth)

    def forward_tile(tile_index):
        row_first, col_first = tile_anchor(tile_index)
        query_tile = take_block(query_feats, row_first, col_first, TILE_ROWS, CC).reshape(-1, head_count, head_dim)
        grad_tile = take_block(cotangent, row_first, col_first, TILE_ROWS, CC).reshape(-1, head_count, head_dim)
        region = take_block(padded_kv, row_first, col_first, region_rows, region_cols).reshape(-1, 2 * feature_count)
        key_region = region[:, :feature_count].reshape(-1, head_count, head_dim)
        value_region = region[:, feature_count:].reshape(-1, head_count, head_dim)
        mixed_out, log_total = attend_tile(query_tile, key_region, value_region, allowed_at(row_first, col_first), key_marks, value_marks, score_scale)
        delta_term = jnp.einsum("qhd,qhd->hq", as_float(grad_tile), mixed_out)
        return mixed_out.astype(jnp.bfloat16), log_total, delta_term

    out_tiles, log_tiles, delta_tiles = lax.map(forward_tile, tile_ids)
    attended = to_grid(out_tiles, feature_count)
    log_grid = to_grid(log_tiles.transpose(0, 2, 1), head_count)
    delta_grid = to_grid(delta_tiles.transpose(0, 2, 1), head_count)

    def query_step(running, tile_index):
        row_first, col_first = tile_anchor(tile_index)
        query_tile = take_block(query_feats, row_first, col_first, TILE_ROWS, CC).reshape(-1, head_count, head_dim)
        grad_tile = take_block(cotangent, row_first, col_first, TILE_ROWS, CC).reshape(-1, head_count, head_dim)
        region = take_block(padded_kv, row_first, col_first, region_rows, region_cols).reshape(-1, 2 * feature_count)
        key_region = region[:, :feature_count].reshape(-1, head_count, head_dim)
        value_region = region[:, feature_count:].reshape(-1, head_count, head_dim)
        log_total = take_block(log_grid, row_first, col_first, TILE_ROWS, CC).reshape(-1, head_count).T
        delta_term = take_block(delta_grid, row_first, col_first, TILE_ROWS, CC).reshape(-1, head_count).T
        grad_q, key_part, value_part = query_grads(query_tile, grad_tile, key_region, value_region, allowed_at(row_first, col_first), key_marks, value_marks, log_total, delta_term, score_scale)
        return (running[0] + key_part, running[1] + value_part), grad_q.astype(jnp.bfloat16)

    zero_marks = jnp.zeros((head_count, mark_count, head_dim), jnp.float32)
    (key_grad_marks, value_grad_marks), query_tiles = lax.scan(query_step, (zero_marks, zero_marks), tile_ids)
    grad_query = to_grid(query_tiles, feature_count)

    padded_qg = jnp.pad(jnp.concatenate([query_feats, cotangent], -1), pad_spec)
    padded_stats = jnp.pad(jnp.concatenate([log_grid, delta_grid], -1), pad_spec)

    def key_tile_grads(tile_index):
        row_first, col_first = tile_anchor(tile_index)
        key_tile = take_block(key_feats, row_first, col_first, TILE_ROWS, CC).reshape(-1, head_count, head_dim)
        value_tile = take_block(value_feats, row_first, col_first, TILE_ROWS, CC).reshape(-1, head_count, head_dim)
        region = take_block(padded_qg, row_first, col_first, region_rows, region_cols).reshape(-1, 2 * feature_count)
        stat_block = take_block(padded_stats, row_first, col_first, region_rows, region_cols).reshape(-1, 2 * head_count)
        query_region = region[:, :feature_count].reshape(-1, head_count, head_dim)
        grad_region = region[:, feature_count:].reshape(-1, head_count, head_dim)
        return key_grads(key_tile, value_tile, query_region, grad_region, allowed_at(row_first, col_first), stat_block[:, :head_count].T, stat_block[:, head_count:].T, score_scale)

    window_k_tiles, window_v_tiles = lax.map(key_tile_grads, tile_ids)
    window_key = to_grid(window_k_tiles, feature_count)
    window_value = to_grid(window_v_tiles, feature_count)

    def landmark_grads(operands):
        key_head, value_head, weight_head, key_mean_h, value_mean_h, key_grad_h, value_grad_h = operands
        logits = jnp.dot(key_head, weight_head, preferred_element_type=jnp.float32)
        exp_terms = jnp.exp(logits - jnp.max(logits, 0))
        land_prob = exp_terms / jnp.sum(exp_terms, 0)
        key_float = as_float(key_head)
        value_float = as_float(value_head)
        prob_grad = jnp.dot(key_float, key_grad_h.T, precision=HIGH_PREC) + jnp.dot(value_float, value_grad_h.T, precision=HIGH_PREC)
        column_term = jnp.sum(key_mean_h * key_grad_h, -1) + jnp.sum(value_mean_h * value_grad_h, -1)
        logit_grad = land_prob * (prob_grad - column_term)
        key_part = jnp.dot(land_prob, key_grad_h, precision=HIGH_PREC) + jnp.dot(logit_grad, as_float(weight_head).T, precision=HIGH_PREC)
        value_part = jnp.dot(land_prob, value_grad_h, precision=HIGH_PREC)
        weight_grad = jnp.dot(key_float.T, logit_grad, precision=HIGH_PREC)
        return key_part, value_part, weight_grad

    key_parts, value_parts, grad_proj = lax.map(landmark_grads, (key_heads, value_heads, proj_weight, key_mean, value_mean, key_grad_marks, value_grad_marks))
    key_land = key_parts.transpose(1, 0, 2).reshape(grid_rows, grid_cols, feature_count)
    value_land = value_parts.transpose(1, 0, 2).reshape(grid_rows, grid_cols, feature_count)
    grad_key = (window_key + key_land).astype(jnp.bfloat16)
    grad_value = (window_value + value_land).astype(jnp.bfloat16)
    return attended, grad_query, grad_key, grad_value, grad_proj
```

```python
import jax
import jax.numpy as jnp
from jax import lax
from jax.experimental import pallas as pl
from jax.experimental.pallas import tpu as pltpu
from jax.sharding import Mesh, PartitionSpec as P

RAD = 8
HEADS = 8
HD = 64
LAND = 256
TOK = 128
STRIP = 384
SCALE = HD**-0.5
NEG = -1e30
BF = jnp.bfloat16
F32 = jnp.float32
GROUP = ("core", "x")
BLOCKS = ("z", "y")
NT = (((1,), (1,)), ((), ()))


def call(body, outs, scratch=(), flops=0, nbytes=0, trans=0, vmem=48):
    return pl.pallas_call(
        body,
        out_shape=outs,
        scratch_shapes=list(scratch),
        compiler_params=pltpu.CompilerParams(vmem_limit_bytes=vmem * 2**20),
        cost_estimate=pl.CostEstimate(flops=flops, bytes_accessed=nbytes, transcendentals=trans),
    )


def dot(a, b, dims=(((1,), (0,)), ((), ()))):
    return lax.dot_general(a, b, dims, preferred_element_type=F32)


def split_hi_lo(x):
    hi = x.astype(BF)
    return hi, (x - hi.astype(F32)).astype(BF)


def pack_kernel(k_ref, v_ref, q_ref, g_ref, out_ref):
    for h in range(HEADS):
        at = slice(h * HD, (h + 1) * HD)
        out_ref[h, 0] = jnp.concatenate([k_ref[:, at], v_ref[:, at]], 1)
        out_ref[h, 1] = jnp.concatenate([q_ref[:, at], g_ref[:, at]], 1)


def final_pack_kernel(out_q_ref, out_kv_ref, proj_ref, out_ref):
    for h in range(HEADS):
        out_ref[h, 0] = out_q_ref[h]
        out_ref[h, 1] = out_kv_ref[h]
        for i in range(2):
            out_ref[h, 2, i * HD : (i + 1) * HD] = proj_ref[pl.ds(i, HD, stride=2), :].astype(BF)


def unpack_kernel(in_ref, att_ref, dq_ref, dk_ref, dv_ref, proj_ref):
    for i in range(HEADS // 2):
        at = slice(i * 2 * HD, (i + 1) * 2 * HD)
        for part, first_ref, second_ref in ((0, att_ref, dq_ref), (1, dk_ref, dv_ref)):
            even, odd = in_ref[2 * i, part], in_ref[2 * i + 1, part]
            first_ref[:, at] = jnp.concatenate([even[:, :HD], odd[:, :HD]], 1)
            second_ref[:, at] = jnp.concatenate([even[:, HD:], odd[:, HD:]], 1)
    for h in range(HEADS):
        proj_ref[h, :, :128] = in_ref[h, 2, :HD].astype(F32)
        proj_ref[h, :, 128:] = in_ref[h, 2, HD:].astype(F32)


def sums_kernel(kvqg_ref, w_ref, out_ref):
    kv = kvqg_ref[:, 0].reshape(HEADS * TOK, 2 * HD)
    logits = dot(w_ref[...], kv, NT)
    top = jnp.max(logits, 1, keepdims=True)
    terms = jnp.exp(logits - top)
    total = jnp.sum(terms, 1, keepdims=True)
    hi, lo = split_hi_lo(terms)
    sums = dot(hi, kv) + dot(lo, kv)
    lane = lax.broadcasted_iota(jnp.int32, (LAND, 2 * HD), 1)
    stats = jnp.where(lane < HD, top, total)
    for j in range(4):
        out_ref[pl.ds(j, 64, stride=8), :] = sums[64 * j : 64 * j + 64]
        out_ref[pl.ds(4 + j, 64, stride=8), :] = stats[64 * j : 64 * j + 64]


def means_kernel(in_ref, out_ref):
    got = in_ref[...]
    stats = pltpu.roll(got, 4, 1)
    other = pltpu.roll(stats, HD, 2)
    low = lax.broadcasted_iota(jnp.int32, got.shape, 2) < HD
    tops = jnp.where(low, stats, other)
    totals = jnp.where(low, other, stats)
    top = jnp.max(tops, 0, keepdims=True)
    factor = jnp.exp(tops - top)
    total = jnp.sum(factor * totals, 0)
    mean = jnp.sum(factor * got, 0) / total
    log_total = top[0] + jnp.log(total)
    row = lax.broadcasted_iota(jnp.int32, mean.shape, 0)
    result = jnp.where(row < 4, mean, pltpu.roll(log_total, 4, 0))
    out_ref[...] = jnp.broadcast_to(result[None], out_ref.shape)


def land_sum_kernel(in_ref, mean_ref, out_ref):
    grads = jnp.sum(in_ref[...], 0)
    mean = mean_ref[0, 0:4]
    column = jnp.broadcast_to(jnp.sum(mean * grads, 1, keepdims=True), grads.shape)
    result = jnp.concatenate([grads, column], 0)
    out_ref[...] = jnp.broadcast_to(result[None], out_ref.shape)


def proj_sum_kernel(in_ref, out_ref):
    out_ref[...] = jnp.broadcast_to(jnp.sum(in_ref[...], 0)[None], out_ref.shape)


def rows_of(ref, first):
    return jnp.concatenate([ref[pl.ds(first + j, 64, stride=8), :] for j in range(4)], 0)


def attend_kernel(
    place_ref, kvqg_ref, top_ref, bottom_ref, left_ref, right_ref, marks_ref,
    out_ref, dkv_ref, dmark_ref,
    ext, ext_t, mask, dmark,
):
    block_row, block_col = place_ref[0], place_ref[1]
    for x in range(4):
        base = (x + 1) * STRIP
        ext[base : base + 64] = top_ref[x]
        ext[base + 64 : base + 192] = kvqg_ref[x, 0]
        ext[base + 192 : base + 320] = kvqg_ref[4 + x, 0]
        ext[base + 320 : base + 384] = bottom_ref[x]
    ext[0:STRIP] = left_ref[...]
    ext[5 * STRIP : 6 * STRIP] = right_ref[...]
    for i in range(18):
        ext_t[:, i * 128 : (i + 1) * 128] = ext[i * 128 : (i + 1) * 128].T
    kv_mark = rows_of(marks_ref, 0).astype(BF)
    kv_mark_t = jnp.concatenate([kv_mark[0:128].T, kv_mark[128:256].T], 1)

    key = lax.broadcasted_iota(jnp.int32, (768, TOK), 0)
    query = lax.broadcasted_iota(jnp.int32, (768, TOK), 1)
    row_gap = ((key >> 3) & 31) - 8 - (query >> 3)
    col_gap = ((key >> 8) - 1) * 8 + (key & 7) - (query & 7)
    near = (row_gap >= -RAD) & (row_gap <= RAD) & (col_gap >= -RAD) & (col_gap <= RAD)
    mask[...] = jnp.where(near, 0.0, NEG)
    dkv_ref[...] = jnp.zeros_like(dkv_ref)
    dmark[...] = jnp.zeros_like(dmark)

    column = lax.broadcasted_iota(jnp.int32, (768, 1), 0)
    key_row, key_slab = (column >> 3) & 31, column >> 8
    lane = lax.broadcasted_iota(jnp.int32, (TOK, 2 * HD), 1)

    def tile(index, carry):
        strip, half = index & 3, index >> 2
        low_row = jnp.where((block_row == 0) & (half == 0), 8, 0)
        high_row = jnp.where((block_row == place_ref[2] - 1) & (half == 1), 24, 32)
        low_slab = jnp.where((block_col == 0) & (strip == 0), 1, 0)
        high_slab = jnp.where((block_col == place_ref[3] - 1) & (strip == 3), 1, 2)
        inside = (key_row >= low_row) & (key_row < high_row) & (key_slab >= low_slab) & (key_slab <= high_slab)
        edge = jnp.where(inside, 0.0, NEG)

        starts = [pl.multiple_of((strip + j) * STRIP + half * TOK, 128) for j in range(3)]
        query_grad = kvqg_ref[index, 1]
        wide = query_grad.astype(F32)
        upper = jnp.where(lane < HD, wide * SCALE, 0.0).astype(BF)
        lower = jnp.where(lane < HD, 0.0, wide).astype(BF)
        pair = jnp.concatenate([upper, lower], 0)
        keys = jnp.concatenate([ext[pl.ds(s, 256), :] for s in starts] + [kv_mark], 0)
        both = dot(keys, pair, NT)
        score = jnp.concatenate([both[:768, :TOK] + (mask[...] + edge), both[768:, :TOK]], 0)
        inner = both[:, TOK:]
        top = jnp.max(score, 0, keepdims=True)
        terms = jnp.exp(score - top)
        prob = terms * (1.0 / jnp.sum(terms, 0, keepdims=True))
        weights = prob.astype(BF)
        slabs_t = [ext_t[:, pl.ds(s, 256)] for s in starts] + [kv_mark_t]
        keys_t = jnp.concatenate(slabs_t, 1)
        mixed = dot(keys_t[HD:], weights)
        grad_t = wide.T[HD:]
        delta = jnp.sum(grad_t * mixed, 0, keepdims=True)
        dscore = (prob * (inner - delta)).astype(BF)
        dquery = dot(keys_t[:HD], dscore) * SCALE
        out_ref[index] = jnp.concatenate([mixed, dquery], 0).T.astype(BF)
        dkv = dot(jnp.concatenate([dscore, weights], 1), pair)
        for j, s in enumerate(starts):
            dkv_ref[pl.ds(s, 256), :] += dkv[256 * j : 256 * j + 256]
        dmark[...] += dkv[768:]
        return carry

    lax.fori_loop(0, 8, tile, 0)
    for j in range(4):
        dmark_ref[pl.ds(j, 64, stride=4), :] = dmark[64 * j : 64 * j + 64]


def land_grad_kernel(kvqg_ref, w_ref, marks_ref, grads_ref, win_ref, out_ref, proj_ref):
    kv = kvqg_ref[:, 0].reshape(HEADS * TOK, 2 * HD)
    weight = w_ref[...]
    log_total = rows_of(marks_ref, 4)[:, :1]
    grads = rows_of(grads_ref, 0)
    column = rows_of(grads_ref, 4)[:, :1]
    prob = jnp.exp(dot(weight, kv, NT) - log_total)
    hi, lo = split_hi_lo(grads)
    dprob = dot(hi, kv, NT) + dot(lo, kv, NT)
    dlogit = prob * (dprob - column)
    dlogit_bf, dlogit_lo = split_hi_lo(dlogit)
    prob_bf, prob_lo = split_hi_lo(prob)
    flip = lambda a: jnp.concatenate([a[:128].T, a[128:].T], 1)
    hi_t, lo_t, weight_t = flip(hi), flip(lo), flip(weight)
    left_t = jnp.concatenate([hi_t, weight_t, hi_t, weight_t, lo_t], 1)
    right = jnp.concatenate([prob_bf, dlogit_bf, prob_lo, dlogit_lo, prob_bf], 0)
    land = dot(left_t, right)
    for i in range(HEADS):
        out_ref[i] = (land[:, i * TOK : (i + 1) * TOK].T + win_ref[i]).astype(BF)
    proj = dot(dlogit_bf, kv) + dot(dlogit_lo, kv)
    for i in range(2):
        proj_ref[pl.ds(i, 64, stride=2), :] = proj[128 * i : 128 * i + 128].T[:HD]


def shape(dims, dtype=F32):
    return jax.ShapeDtypeStruct(dims, dtype)


def swap(x, axes):
    return lax.all_to_all(x, axes, 0, 0, tiled=True)


def shift(x, axis, step):
    n = lax.axis_size(axis)
    return lax.ppermute(x, axis, [(i, i + step) for i in range(n) if 0 <= i + step < n])


def per_device(query_feats, key_feats, value_feats, proj_weight, cotangent):
    rows, cols, feats = query_feats.shape
    flat = lambda a: a.reshape(TOK, feats)
    head = lax.axis_index("core") * lax.axis_size("x") + lax.axis_index("x")
    weight = lax.dynamic_index_in_dim(proj_weight, head, 0, keepdims=False)
    weight = jnp.pad(weight.T, ((0, 0), (0, HD)))
    place = jnp.stack(
        [lax.axis_index("z"), lax.axis_index("y"), lax.axis_size("z"), lax.axis_size("y")]
    ).astype(jnp.int32)

    packed = call(pack_kernel, shape((HEADS, 2, TOK, 2 * HD), BF), nbytes=2**20)(
        flat(key_feats), flat(value_feats), flat(query_feats), flat(cotangent)
    )
    own = swap(packed, GROUP)

    sums = call(sums_kernel, shape((512, 128)), flops=2 * 3 * 2**25, nbytes=2**19, trans=2**18)(own, weight)

    top = shift(own[4:8, 0, 64:], "z", 1)
    bottom = shift(own[0:4, 0, :64], "z", -1)
    strip_of = lambda x: jnp.concatenate([top[x], own[x, 0], own[4 + x, 0], bottom[x]], 0)
    left = shift(strip_of(3), "y", 1)
    right = shift(strip_of(0), "y", -1)

    mean = call(means_kernel, shape((64, 8, 128)), nbytes=2**19)(swap(sums.reshape(64, 8, 128), BLOCKS))
    marks = swap(mean, BLOCKS).reshape(512, 128)

    out_q, dkv, dmark = pl.pallas_call(
        attend_kernel,
        in_specs=[pl.BlockSpec(memory_space=pltpu.SMEM)] + [pl.BlockSpec(memory_space=pltpu.VMEM)] * 6,
        out_shape=(shape((HEADS, TOK, 2 * HD), BF), shape((6 * STRIP, 2 * HD)), shape((256, 128))),
        scratch_shapes=[
            pltpu.VMEM((6 * STRIP, 2 * HD), BF),
            pltpu.VMEM((2 * HD, 6 * STRIP), BF),
            pltpu.VMEM((768, TOK), F32),
            pltpu.VMEM((LAND, 2 * HD), F32),
        ],
        compiler_params=pltpu.CompilerParams(vmem_limit_bytes=48 * 2**20),
        cost_estimate=pl.CostEstimate(flops=2**32, bytes_accessed=2**22, transcendentals=2**20),
    )(place, own, top, bottom, left, right, marks)

    grads = call(land_sum_kernel, shape((64, 8, 128)), nbytes=2**19)(
        swap(dmark.reshape(64, 4, 128), BLOCKS), mean
    )
    grads = swap(grads, BLOCKS).reshape(512, 128)

    dkv = dkv.reshape(6, STRIP, 2 * HD)
    from_right = shift(dkv[0].astype(BF), "y", -1)
    from_left = shift(dkv[5].astype(BF), "y", 1)
    first = dkv[1] + from_left.astype(F32)
    last = dkv[4] + from_right.astype(F32)
    strips = jnp.stack([first, dkv[2], dkv[3], last])
    from_below = shift(strips[:, :64].astype(BF), "z", -1)
    from_above = shift(strips[:, 320:].astype(BF), "z", 1)
    upper = strips[:, 64:192].at[:, :64].add(from_above.astype(F32))
    lower = strips[:, 192:320].at[:, 64:].add(from_below.astype(F32))
    window = jnp.concatenate([upper, lower], 0)

    out_kv, proj = call(
        land_grad_kernel,
        (shape((HEADS, TOK, 2 * HD), BF), shape((128, 128))),
        flops=2 * 8 * 2**25, nbytes=2**20, trans=2**18,
    )(own, weight, marks, grads, window)
    proj = call(proj_sum_kernel, shape((64, 2, 128)))(swap(proj.reshape(64, 2, 128), BLOCKS))
    proj = swap(proj, BLOCKS).reshape(128, 128)
    final = call(final_pack_kernel, shape((HEADS, 3, TOK, 128), BF), nbytes=2**20)(out_q, out_kv, proj)
    *tokens, grad_proj = call(
        unpack_kernel,
        (shape((TOK, feats), BF),) * 4 + (shape((HEADS, HD, LAND)),),
        nbytes=2**20,
    )(swap(final, GROUP))
    return *(a.reshape(rows, cols, feats) for a in tokens), grad_proj


def solution(mesh):
    total_rows, total_cols = mesh.devices.shape
    fine = Mesh(mesh.devices.reshape(total_rows // 2, 2, total_cols // 4, 4), ("z", "core", "y", "x"))
    tokens = P(("z", "core"), ("y", "x"), None)
    return jax.shard_map(
        per_device,
        mesh=fine,
        in_specs=(tokens, tokens, tokens, P(), tokens),
        out_specs=(tokens, tokens, tokens, tokens, P()),
        check_vma=False,
    )
```

```python
import jax
import jax.numpy as jnp
from jax import lax
from jax.experimental import pallas as pl
from jax.experimental.pallas import tpu as pltpu
from jax.sharding import Mesh, PartitionSpec as P

RAD = 8
HEADS = 8
HD = 64
LAND = 256
TOK = 128
STRIP = 384
SCALE = HD**-0.5
NEG = -1e30
VMEM = 24 * 2**20
PACK_VMEM = 2**26 - 2**18
BF = jnp.bfloat16
F32 = jnp.float32
GROUP = ("core", "x")
BLOCKS = ("z", "y")
NT = (((1,), (1,)), ((), ()))


def call(body, outs, flops=0, nbytes=0, trans=0, after=()):
    def ordered(*refs):
        return body(*refs[len(after) :])

    return lambda *args: pl.pallas_call(
        ordered,
        out_shape=outs,
        in_specs=[pl.BlockSpec(memory_space=pl.ANY)] * len(after)
        + [pl.BlockSpec(memory_space=pltpu.VMEM)] * len(args),
        compiler_params=pltpu.CompilerParams(vmem_limit_bytes=VMEM),
        cost_estimate=pl.CostEstimate(flops=flops, bytes_accessed=nbytes, transcendentals=trans),
    )(*after, *args)


def dot(a, b, dims=(((1,), (0,)), ((), ()))):
    return lax.dot_general(a, b, dims, preferred_element_type=F32)


def split_hi_lo(x):
    hi = x.astype(BF)
    return hi, (x - hi.astype(F32)).astype(BF)


def pack_kernel(k_hbm, v_hbm, q_hbm, g_hbm, out_ref, held, sems):
    copies = [
        pltpu.make_async_copy(source, held.at[i], sems.at[i])
        for i, source in enumerate((k_hbm, v_hbm, q_hbm, g_hbm))
    ]
    for copy in copies:
        copy.start()
    for copy in copies:
        copy.wait()
    for h in range(HEADS):
        at = slice(h * HD, (h + 1) * HD)
        for part in range(2):
            out_ref[h, part] = jnp.concatenate([held[2 * part, :, at], held[2 * part + 1, :, at]], 1)


def final_pack_kernel(out_q_ref, land_ref, dkv_ref, left_ref, right_ref, above_ref, below_ref, proj_ref, out_ref):
    proj = sum_of_eight(proj_ref)
    for h in range(HEADS):
        half, strip = h // 4, h % 4
        base = (strip + 1) * STRIP + 64 + half * TOK
        grads = land_ref[h] + dkv_ref[base : base + TOK]
        if strip == 0:
            grads += left_ref[64 + half * TOK : 64 + half * TOK + TOK].astype(F32)
        if strip == 3:
            grads += right_ref[64 + half * TOK : 64 + half * TOK + TOK].astype(F32)
        zero = jnp.zeros((64, 2 * HD), F32)
        if half == 0:
            grads += jnp.concatenate([above_ref[strip].astype(F32), zero], 0)
        else:
            grads += jnp.concatenate([zero, below_ref[strip].astype(F32)], 0)
        out_ref[h, 0] = out_q_ref[h]
        out_ref[h, 1] = grads.astype(BF)
        out_ref[h, 2] = proj


def edge_kernel(dkv_ref, left_ref, right_ref, top_ref, bottom_ref):
    for strip in range(4):
        base = (strip + 1) * STRIP
        for ref, first in ((top_ref, 0), (bottom_ref, 320)):
            grads = dkv_ref[base + first : base + first + 64]
            if strip == 0:
                grads += left_ref[first : first + 64].astype(F32)
            if strip == 3:
                grads += right_ref[first : first + 64].astype(F32)
            ref[strip] = grads.astype(BF)


def unpack_kernel(in_ref, att_ref, dq_ref, dk_ref, dv_ref, proj_ref):
    for i in range(HEADS // 2):
        at = slice(i * 2 * HD, (i + 1) * 2 * HD)
        for part, first_ref, second_ref in ((0, att_ref, dq_ref), (1, dk_ref, dv_ref)):
            even, odd = in_ref[2 * i, part], in_ref[2 * i + 1, part]
            first_ref[:, at] = jnp.concatenate([even[:, :HD], odd[:, :HD]], 1)
            second_ref[:, at] = jnp.concatenate([even[:, HD:], odd[:, HD:]], 1)
    for h in range(HEADS):
        proj_ref[h, :, :128] = in_ref[h, 2, :HD].astype(F32)
        proj_ref[h, :, 128:] = in_ref[h, 2, HD:].astype(F32)


def sums_kernel(kvqg_ref, w_ref, out_ref):
    kv = kvqg_ref[:, 0].reshape(HEADS * TOK, 2 * HD)
    logits = dot(w_ref[...], kv, NT)
    top = jnp.max(logits, 1, keepdims=True)
    terms = jnp.exp(logits - top)
    total = jnp.sum(terms, 1, keepdims=True)
    hi, lo = split_hi_lo(terms)
    sums = dot(hi, kv) + dot(lo, kv)
    lane = lax.broadcasted_iota(jnp.int32, (LAND, 2 * HD), 1)
    stats = jnp.where(lane < HD, top, total)
    for j in range(4):
        out_ref[pl.ds(j, 64, stride=8), :] = sums[64 * j : 64 * j + 64]
        out_ref[pl.ds(4 + j, 64, stride=8), :] = stats[64 * j : 64 * j + 64]


def means_kernel(in_ref, out_ref, own_ref):
    got = in_ref[...]
    stats = pltpu.roll(got, 4, 1)
    other = pltpu.roll(stats, HD, 2)
    low = lax.broadcasted_iota(jnp.int32, got.shape, 2) < HD
    tops = jnp.where(low, stats, other)
    totals = jnp.where(low, other, stats)
    top = jnp.max(tops, 0, keepdims=True)
    factor = jnp.exp(tops - top)
    total = jnp.sum(factor * totals, 0)
    mean = jnp.sum(factor * got, 0) / total
    log_total = top[0] + jnp.log(total)
    row = lax.broadcasted_iota(jnp.int32, mean.shape, 0)
    result = jnp.where(row < 4, mean, pltpu.roll(log_total, 4, 0))
    own_ref[...] = result
    out_ref[...] = jnp.broadcast_to(result[None], out_ref.shape)


def land_sum_kernel(in_ref, mean_ref, out_ref):
    grads = jnp.sum(in_ref[...].reshape(32, 8, 2 * HD), 0)
    grads = grads + pltpu.roll(grads, 4, 0)
    column = jnp.sum(mean_ref[...] * grads, 1, keepdims=True)
    row = lax.broadcasted_iota(jnp.int32, grads.shape, 0)
    column = pltpu.roll(jnp.broadcast_to(column, grads.shape), 4, 0)
    result = jnp.where(row < 4, grads, column)
    out_ref[...] = jnp.broadcast_to(result[None], out_ref.shape)


def sum_of_eight(in_ref):
    total = in_ref[0].astype(F32)
    for i in range(1, 8):
        total += in_ref[i].astype(F32)
    return total.astype(BF)


def proj_sum_kernel(in_ref, out_ref):
    out_ref[...] = jnp.broadcast_to(sum_of_eight(in_ref)[None], out_ref.shape)


def rows_of(ref, first):
    return jnp.concatenate([ref[pl.ds(first + j, 64, stride=8), :] for j in range(4)], 0)


def fill_mask(mask):
    key = lax.broadcasted_iota(jnp.int32, (768, TOK), 0)
    query = lax.broadcasted_iota(jnp.int32, (768, TOK), 1)
    row_gap = ((key >> 3) & 31) - 8 - (query >> 3)
    col_gap = ((key >> 8) - 1) * 8 + (key & 7) - (query & 7)
    near = (row_gap >= -RAD) & (row_gap <= RAD) & (col_gap >= -RAD) & (col_gap <= RAD)
    mask[...] = jnp.where(near, 0.0, NEG)


def edge_bias(place_ref, strip, half):
    column = lax.broadcasted_iota(jnp.int32, (768, 1), 0)
    key_row, key_slab = (column >> 3) & 31, column >> 8
    low_row = jnp.where((place_ref[0] == 0) & (half == 0), 8, 0)
    high_row = jnp.where((place_ref[0] == place_ref[2] - 1) & (half == 1), 24, 32)
    low_slab = jnp.where((place_ref[1] == 0) & (strip == 0), 1, 0)
    high_slab = jnp.where((place_ref[1] == place_ref[3] - 1) & (strip == 3), 1, 2)
    inside = (key_row >= low_row) & (key_row < high_row) & (key_slab >= low_slab) & (key_slab <= high_slab)
    return jnp.where(inside, 0.0, NEG)


def query_pair(query_grad):
    lane = lax.broadcasted_iota(jnp.int32, (TOK, 2 * HD), 1)
    wide = query_grad.astype(F32)
    upper = jnp.where(lane < HD, wide * SCALE, 0.0).astype(BF)
    lower = jnp.where(lane < HD, 0.0, wide).astype(BF)
    return wide, jnp.concatenate([upper, lower], 0)


def slab_starts(strip, half):
    return [pl.multiple_of((strip + j) * STRIP + half * TOK, 128) for j in range(3)]


def fill_region(kvqg_ref, top_ref, bottom_ref, left_ref, right_ref, ext, ext_t):
    for x in range(4):
        base = (x + 1) * STRIP
        ext[base : base + 64] = top_ref[x]
        ext[base + 64 : base + 192] = kvqg_ref[x, 0]
        ext[base + 192 : base + 320] = kvqg_ref[4 + x, 0]
        ext[base + 320 : base + 384] = bottom_ref[x]
    ext[0:STRIP] = left_ref[...]
    ext[5 * STRIP : 6 * STRIP] = right_ref[...]
    for i in range(18):
        ext_t[:, i * 128 : (i + 1) * 128] = ext[i * 128 : (i + 1) * 128].T


def forward_kernel(
    place_ref, kvqg_ref, top_ref, bottom_ref, left_ref, right_ref, marks_ref,
    part_ref, stat_ref, dmark_ref,
    ext, ext_t, mask, dmark,
):
    fill_region(kvqg_ref, top_ref, bottom_ref, left_ref, right_ref, ext, ext_t)
    kv_mark = rows_of(marks_ref, 0).astype(BF)
    kv_mark_t = jnp.concatenate([kv_mark[0:128].T, kv_mark[128:256].T], 1)
    fill_mask(mask)
    dmark[...] = jnp.zeros_like(dmark)

    def tile(index, carry):
        strip, half = index & 3, index >> 2
        starts = slab_starts(strip, half)
        wide, pair = query_pair(kvqg_ref[index, 1])
        near_keys = jnp.concatenate([ext[pl.ds(s, 256), :] for s in starts], 0)
        near_score = dot(near_keys, pair[:TOK], NT) + (mask[...] + edge_bias(place_ref, strip, half))
        both = dot(kv_mark, pair, NT)
        mark_score, mark_inner = both[:, :TOK], both[:, TOK:]
        top = jnp.maximum(
            jnp.max(near_score, 0, keepdims=True), jnp.max(mark_score, 0, keepdims=True)
        )
        near_terms, mark_terms = jnp.exp(near_score - top), jnp.exp(mark_score - top)
        total = jnp.sum(near_terms, 0, keepdims=True) + jnp.sum(mark_terms, 0, keepdims=True)
        share = 1.0 / total
        prob = mark_terms * share
        weights = prob.astype(BF)
        near_weights = (near_terms * share).astype(BF)
        slabs_t = jnp.concatenate([ext_t[HD:, pl.ds(s, 256)] for s in starts] + [kv_mark_t[HD:]], 1)
        mixed = dot(slabs_t, jnp.concatenate([near_weights, weights], 0))
        delta = jnp.sum(wide.T[HD:] * mixed, 0, keepdims=True)
        dscore = (prob * (mark_inner - delta)).astype(BF)
        part_ref[index] = jnp.concatenate([mixed, dot(kv_mark_t[:HD], dscore)], 0).astype(BF)
        stat_ref[index] = jnp.concatenate([top + jnp.log(total), delta], 0)
        dmark[...] += dot(jnp.concatenate([dscore, weights], 1), pair)
        return carry

    lax.fori_loop(0, 8, tile, 0, unroll=2)
    for j in range(4):
        dmark_ref[pl.ds(j, 64, stride=4), :] = dmark[64 * j : 64 * j + 64]


def window_kernel(
    place_ref, kvqg_ref, top_ref, bottom_ref, left_ref, right_ref, part_ref, stat_ref,
    out_ref, dkv_ref, side_ref,
    ext, ext_t, mask,
):
    fill_region(kvqg_ref, top_ref, bottom_ref, left_ref, right_ref, ext, ext_t)
    fill_mask(mask)
    dkv_ref[...] = jnp.zeros_like(dkv_ref)

    def tile(index, carry):
        strip, half = index & 3, index >> 2
        starts = slab_starts(strip, half)
        _, pair = query_pair(kvqg_ref[index, 1])
        stats = stat_ref[index]
        both = dot(jnp.concatenate([ext[pl.ds(s, 256), :] for s in starts], 0), pair, NT)
        score = both[:, :TOK] + (mask[...] + edge_bias(place_ref, strip, half))
        prob = jnp.exp(score - stats[0:1])
        dscore = (prob * (both[:, TOK:] - stats[1:2])).astype(BF)
        slabs_t = jnp.concatenate([ext_t[:HD, pl.ds(s, 256)] for s in starts], 1)
        part = part_ref[index].astype(F32)
        dquery = (dot(slabs_t, dscore) + part[HD:]) * SCALE
        out_ref[index] = jnp.concatenate([part[:HD], dquery], 0).T.astype(BF)
        dkv = dot(jnp.concatenate([dscore, prob.astype(BF)], 1), pair)
        for j, s in enumerate(starts):
            dkv_ref[pl.ds(s, 256), :] += dkv[256 * j : 256 * j + 256]
        return carry

    lax.fori_loop(0, 8, tile, 0, unroll=2)
    side_ref[0] = dkv_ref[0:STRIP].astype(BF)
    side_ref[1] = dkv_ref[5 * STRIP : 6 * STRIP].astype(BF)


def land_grad_kernel(kvqg_ref, w_ref, marks_ref, grads_ref, out_ref, proj_ref):
    kv = kvqg_ref[:, 0].reshape(HEADS * TOK, 2 * HD)
    weight = w_ref[...]
    log_total = rows_of(marks_ref, 4)[:, :1]
    grads = rows_of(grads_ref, 0)
    column = rows_of(grads_ref, 4)[:, :1]
    prob = jnp.exp(dot(weight, kv, NT) - log_total)
    hi, lo = split_hi_lo(grads)
    dprob = dot(hi, kv, NT) + dot(lo, kv, NT)
    dlogit = prob * (dprob - column)
    dlogit_bf, dlogit_lo = split_hi_lo(dlogit)
    prob_bf, prob_lo = split_hi_lo(prob)
    flip = lambda a: jnp.concatenate([a[:128].T, a[128:].T], 1)
    hi_t, lo_t, weight_t = flip(hi), flip(lo), flip(weight)
    left_t = jnp.concatenate([hi_t, weight_t, hi_t, weight_t, lo_t], 1)
    right = jnp.concatenate([prob_bf, dlogit_bf, prob_lo, dlogit_lo, prob_bf], 0)
    land = dot(left_t, right)
    for i in range(HEADS):
        out_ref[i] = land[:, i * TOK : (i + 1) * TOK].T
    proj = dot(dlogit_bf, kv) + dot(dlogit_lo, kv)
    proj = jnp.concatenate([proj[128 * i : 128 * i + 128].T[:HD] for i in range(2)], 0)
    proj_ref[...] = jnp.broadcast_to(proj.astype(BF)[None], proj_ref.shape)


def shape(dims, dtype=F32):
    return jax.ShapeDtypeStruct(dims, dtype)


def swap(x, axes):
    return lax.all_to_all(x, axes, 0, 0, tiled=True)


def shift(x, axis, step):
    n = lax.axis_size(axis)
    return lax.ppermute(x, axis, [(i, i + step) for i in range(n) if 0 <= i + step < n])


def per_device(query_feats, key_feats, value_feats, proj_weight, cotangent):
    rows, cols, feats = query_feats.shape
    flat = lambda a: a.reshape(TOK, feats)
    head = lax.axis_index("core") * lax.axis_size("x") + lax.axis_index("x")
    weight = lax.dynamic_index_in_dim(proj_weight, head, 0, keepdims=False)
    weight = jnp.pad(weight.T, ((0, 0), (0, HD)))
    place = jnp.stack(
        [lax.axis_index("z"), lax.axis_index("y"), lax.axis_size("z"), lax.axis_size("y")]
    ).astype(jnp.int32)

    packed = pl.pallas_call(
        pack_kernel,
        in_specs=[pl.BlockSpec(memory_space=pltpu.HBM)] * 4,
        out_shape=shape((HEADS, 2, TOK, 2 * HD), BF),
        scratch_shapes=[pltpu.VMEM((4, TOK, feats), BF), pltpu.SemaphoreType.DMA((4,))],
        compiler_params=pltpu.CompilerParams(vmem_limit_bytes=PACK_VMEM),
        cost_estimate=pl.CostEstimate(flops=0, bytes_accessed=2**20, transcendentals=0),
    )(flat(key_feats), flat(value_feats), flat(query_feats), flat(cotangent))
    own = swap(packed, GROUP)

    sums = call(sums_kernel, shape((512, 128)), flops=2 * 3 * 2**25, nbytes=2**19, trans=2**18)(own, weight)

    top = shift(own[4:8, 0, 64:], "z", 1)
    bottom = shift(own[0:4, 0, :64], "z", -1)
    strip_of = lambda x: jnp.concatenate([top[x], own[x, 0], own[4 + x, 0], bottom[x]], 0)
    left = shift(strip_of(3), "y", 1)
    right = shift(strip_of(0), "y", -1)

    means, mean = call(means_kernel, (shape((64, 8, 128)), shape((8, 128))), nbytes=2**19)(
        swap(sums.reshape(64, 8, 128), BLOCKS)
    )
    marks = swap(means, BLOCKS).reshape(512, 128)

    smem, vmem = pl.BlockSpec(memory_space=pltpu.SMEM), pl.BlockSpec(memory_space=pltpu.VMEM)
    region = [
        pltpu.VMEM((6 * STRIP, 2 * HD), BF),
        pltpu.VMEM((2 * HD, 6 * STRIP), BF),
        pltpu.VMEM((768, TOK), F32),
    ]
    part, stats, dmark = pl.pallas_call(
        forward_kernel,
        in_specs=[smem] + [vmem] * 6,
        out_shape=(
            shape((HEADS, 2 * HD, TOK), BF),
            shape((HEADS, 2, TOK)),
            shape((LAND, 2 * HD)),
        ),
        scratch_shapes=region + [pltpu.VMEM((LAND, 2 * HD), F32)],
        compiler_params=pltpu.CompilerParams(vmem_limit_bytes=VMEM),
        cost_estimate=pl.CostEstimate(flops=2**31, bytes_accessed=2**22, transcendentals=2**20),
    )(place, own, top, bottom, left, right, marks)

    out_q, dkv, sides = pl.pallas_call(
        window_kernel,
        in_specs=[smem] + [vmem] * 7,
        out_shape=(
            shape((HEADS, TOK, 2 * HD), BF),
            shape((6 * STRIP, 2 * HD)),
            shape((2, STRIP, 2 * HD), BF),
        ),
        scratch_shapes=region,
        compiler_params=pltpu.CompilerParams(vmem_limit_bytes=VMEM),
        cost_estimate=pl.CostEstimate(flops=2**32, bytes_accessed=2**22, transcendentals=2**20),
    )(place, own, top, bottom, left, right, part, stats)
    from_right = shift(sides[0], "y", -1)
    from_left = shift(sides[1], "y", 1)
    to_above, to_below = call(edge_kernel, (shape((4, 64, 2 * HD), BF),) * 2, nbytes=2**18)(
        dkv, from_left, from_right
    )
    from_below = shift(to_above, "z", -1)
    from_above = shift(to_below, "z", 1)

    grads = call(land_sum_kernel, shape((64, 8, 128)), nbytes=2**19, after=(sides,))(
        swap(dmark.reshape(64, 4, 128), BLOCKS).reshape(256, 128), mean
    )
    grads = swap(grads, BLOCKS).reshape(512, 128)

    land, proj = call(
        land_grad_kernel,
        (shape((HEADS, TOK, 2 * HD)), shape((8, 128, 128), BF)),
        flops=2 * 8 * 2**25, nbytes=2**20, trans=2**18, after=(to_above, to_below),
    )(own, weight, marks, grads)
    proj = swap(call(proj_sum_kernel, shape((8, 128, 128), BF))(swap(proj, "z")), "y")
    final = call(final_pack_kernel, shape((HEADS, 3, TOK, 128), BF), nbytes=2**20)(
        out_q, land, dkv, from_left, from_right, from_above, from_below, proj
    )
    *tokens, grad_proj = call(
        unpack_kernel,
        (shape((TOK, feats), BF),) * 4 + (shape((HEADS, HD, LAND)),),
        nbytes=2**20,
    )(swap(final, GROUP))
    return *(a.reshape(rows, cols, feats) for a in tokens), grad_proj


def solution(mesh):
    total_rows, total_cols = mesh.devices.shape
    fine = Mesh(mesh.devices.reshape(total_rows // 2, 2, total_cols // 4, 4), ("z", "core", "y", "x"))
    tokens = P(("z", "core"), ("y", "x"), None)
    return jax.shard_map(
        per_device,
        mesh=fine,
        in_specs=(tokens, tokens, tokens, P(), tokens),
        out_specs=(tokens, tokens, tokens, tokens, P()),
        check_vma=False,
    )
```

```python
import jax
import jax.numpy as jnp
from jax import lax
from jax.experimental import pallas as pl
from jax.experimental.pallas import tpu as pltpu
from jax.sharding import Mesh, PartitionSpec as P

RAD = 8
HEADS = 8
HD = 64
LAND = 256
TOK = 128
STRIP = 384
SCALE = HD**-0.5
NEG = -1e30
VMEM = 24 * 2**20
PACK_VMEM = 2**26 - 2**18
BF = jnp.bfloat16
F32 = jnp.float32
GROUP = ("core", "x")
BLOCKS = ("z", "y")
NT = (((1,), (1,)), ((), ()))


def call(body, outs, flops=0, nbytes=0, trans=0, after=()):
    def ordered(*refs):
        return body(*refs[len(after) :])

    return lambda *args: pl.pallas_call(
        ordered,
        out_shape=outs,
        in_specs=[pl.BlockSpec(memory_space=pl.ANY)] * len(after)
        + [pl.BlockSpec(memory_space=pltpu.VMEM)] * len(args),
        compiler_params=pltpu.CompilerParams(vmem_limit_bytes=VMEM),
        cost_estimate=pl.CostEstimate(flops=flops, bytes_accessed=nbytes, transcendentals=trans),
    )(*after, *args)


def dot(a, b, dims=(((1,), (0,)), ((), ()))):
    return lax.dot_general(a, b, dims, preferred_element_type=F32)


def split_hi_lo(x):
    hi = x.astype(BF)
    return hi, (x - hi.astype(F32)).astype(BF)


def pack_kernel(k_hbm, v_hbm, q_hbm, g_hbm, out_ref, held, sems):
    copies = [
        pltpu.make_async_copy(source, held.at[i], sems.at[i])
        for i, source in enumerate((k_hbm, v_hbm, q_hbm, g_hbm))
    ]
    for copy in copies:
        copy.start()
    for copy in copies:
        copy.wait()
    for h in range(HEADS):
        at = slice(h * HD, (h + 1) * HD)
        for part in range(2):
            out_ref[h, part] = jnp.concatenate([held[2 * part, :, at], held[2 * part + 1, :, at]], 1)


def final_pack_kernel(out_q_ref, land_ref, dkv_ref, left_ref, right_ref, above_ref, below_ref, proj_ref, out_ref):
    proj = sum_of_eight(proj_ref)
    for h in range(HEADS):
        half, strip = h // 4, h % 4
        base = (strip + 1) * STRIP + 64 + half * TOK
        grads = land_ref[h] + dkv_ref[base : base + TOK]
        if strip == 0:
            grads += left_ref[64 + half * TOK : 64 + half * TOK + TOK].astype(F32)
        if strip == 3:
            grads += right_ref[64 + half * TOK : 64 + half * TOK + TOK].astype(F32)
        zero = jnp.zeros((64, 2 * HD), F32)
        if half == 0:
            grads += jnp.concatenate([above_ref[strip].astype(F32), zero], 0)
        else:
            grads += jnp.concatenate([zero, below_ref[strip].astype(F32)], 0)
        out_ref[h, 0] = out_q_ref[h]
        out_ref[h, 1] = grads.astype(BF)
        out_ref[h, 2] = proj


def edge_kernel(dkv_ref, left_ref, right_ref, top_ref, bottom_ref):
    for strip in range(4):
        base = (strip + 1) * STRIP
        for ref, first in ((top_ref, 0), (bottom_ref, 320)):
            grads = dkv_ref[base + first : base + first + 64]
            if strip == 0:
                grads += left_ref[first : first + 64].astype(F32)
            if strip == 3:
                grads += right_ref[first : first + 64].astype(F32)
            ref[strip] = grads.astype(BF)


def unpack_kernel(in_ref, att_ref, dq_ref, dk_ref, dv_ref, proj_ref):
    for i in range(HEADS // 2):
        at = slice(i * 2 * HD, (i + 1) * 2 * HD)
        for part, first_ref, second_ref in ((0, att_ref, dq_ref), (1, dk_ref, dv_ref)):
            even, odd = in_ref[2 * i, part], in_ref[2 * i + 1, part]
            first_ref[:, at] = jnp.concatenate([even[:, :HD], odd[:, :HD]], 1)
            second_ref[:, at] = jnp.concatenate([even[:, HD:], odd[:, HD:]], 1)
    for h in range(HEADS):
        proj_ref[h, :, :128] = in_ref[h, 2, :HD].astype(F32)
        proj_ref[h, :, 128:] = in_ref[h, 2, HD:].astype(F32)


def sums_kernel(kvqg_ref, w_ref, out_ref):
    kv = kvqg_ref[:, 0].reshape(HEADS * TOK, 2 * HD)
    logits = dot(w_ref[...], kv, NT)
    top = jnp.max(logits, 1, keepdims=True)
    terms = jnp.exp(logits - top)
    total = jnp.sum(terms, 1, keepdims=True)
    hi, lo = split_hi_lo(terms)
    sums = dot(hi, kv) + dot(lo, kv)
    lane = lax.broadcasted_iota(jnp.int32, (LAND, 2 * HD), 1)
    stats = jnp.where(lane < HD, top, total)
    for j in range(4):
        out_ref[pl.ds(j, 64, stride=8), :] = sums[64 * j : 64 * j + 64]
        out_ref[pl.ds(4 + j, 64, stride=8), :] = stats[64 * j : 64 * j + 64]


def means_kernel(in_ref, out_ref, own_ref):
    got = in_ref[...]
    stats = pltpu.roll(got, 4, 1)
    other = pltpu.roll(stats, HD, 2)
    low = lax.broadcasted_iota(jnp.int32, got.shape, 2) < HD
    tops = jnp.where(low, stats, other)
    totals = jnp.where(low, other, stats)
    top = jnp.max(tops, 0, keepdims=True)
    factor = jnp.exp(tops - top)
    total = jnp.sum(factor * totals, 0)
    mean = jnp.sum(factor * got, 0) / total
    log_total = top[0] + jnp.log(total)
    row = lax.broadcasted_iota(jnp.int32, mean.shape, 0)
    result = jnp.where(row < 4, mean, pltpu.roll(log_total, 4, 0))
    own_ref[...] = result
    out_ref[...] = jnp.broadcast_to(result[None], out_ref.shape)


def land_sum_kernel(in_ref, mean_ref, out_ref):
    grads = jnp.sum(in_ref[...].reshape(32, 8, 2 * HD), 0)
    grads = grads + pltpu.roll(grads, 4, 0)
    column = jnp.sum(mean_ref[...] * grads, 1, keepdims=True)
    row = lax.broadcasted_iota(jnp.int32, grads.shape, 0)
    column = pltpu.roll(jnp.broadcast_to(column, grads.shape), 4, 0)
    result = jnp.where(row < 4, grads, column)
    out_ref[...] = jnp.broadcast_to(result[None], out_ref.shape)


def sum_of_eight(in_ref):
    total = in_ref[0].astype(F32)
    for i in range(1, 8):
        total += in_ref[i].astype(F32)
    return total.astype(BF)


def proj_sum_kernel(in_ref, out_ref):
    out_ref[...] = jnp.broadcast_to(sum_of_eight(in_ref)[None], out_ref.shape)


def rows_of(ref, first):
    return jnp.concatenate([ref[pl.ds(first + j, 64, stride=8), :] for j in range(4)], 0)


def fill_mask(mask):
    key = lax.broadcasted_iota(jnp.int32, (768, TOK), 0)
    query = lax.broadcasted_iota(jnp.int32, (768, TOK), 1)
    row_gap = ((key >> 3) & 31) - 8 - (query >> 3)
    col_gap = ((key >> 8) - 1) * 8 + (key & 7) - (query & 7)
    near = (row_gap >= -RAD) & (row_gap <= RAD) & (col_gap >= -RAD) & (col_gap <= RAD)
    mask[...] = jnp.where(near, 0.0, NEG)


def edge_bias(place_ref, strip, half):
    column = lax.broadcasted_iota(jnp.int32, (768, 1), 0)
    key_row, key_slab = (column >> 3) & 31, column >> 8
    low_row = jnp.where((place_ref[0] == 0) & (half == 0), 8, 0)
    high_row = jnp.where((place_ref[0] == place_ref[2] - 1) & (half == 1), 24, 32)
    low_slab = jnp.where((place_ref[1] == 0) & (strip == 0), 1, 0)
    high_slab = jnp.where((place_ref[1] == place_ref[3] - 1) & (strip == 3), 1, 2)
    inside = (key_row >= low_row) & (key_row < high_row) & (key_slab >= low_slab) & (key_slab <= high_slab)
    return jnp.where(inside, 0.0, NEG)


def query_pair(query_grad):
    lane = lax.broadcasted_iota(jnp.int32, (TOK, 2 * HD), 1)
    wide = query_grad.astype(F32)
    upper = jnp.where(lane < HD, wide * SCALE, 0.0).astype(BF)
    lower = jnp.where(lane < HD, 0.0, wide).astype(BF)
    return wide, jnp.concatenate([upper, lower], 0)


def slab_starts(strip, half):
    return [pl.multiple_of((strip + j) * STRIP + half * TOK, 128) for j in range(3)]


def fill_strip(kvqg_ref, top_ref, bottom_ref, ext, x, base):
    ext[base : base + 64] = top_ref[x]
    ext[base + 64 : base + 192] = kvqg_ref[x, 0]
    ext[base + 192 : base + 320] = kvqg_ref[4 + x, 0]
    ext[base + 320 : base + 384] = bottom_ref[x]


def fill_region(kvqg_ref, top_ref, bottom_ref, left_ref, right_ref, ext, ext_t):
    for x in range(4):
        fill_strip(kvqg_ref, top_ref, bottom_ref, ext, x, (x + 1) * STRIP)
    ext[0:STRIP] = left_ref[...]
    ext[5 * STRIP : 6 * STRIP] = right_ref[...]
    for i in range(18):
        ext_t[:, i * 128 : (i + 1) * 128] = ext[i * 128 : (i + 1) * 128].T


def near_kernel(place_ref, kvqg_ref, top_ref, bottom_ref, near_ref, stat_ref, ext, ext_t, mask):
    for x in range(4):
        fill_strip(kvqg_ref, top_ref, bottom_ref, ext, x, x * STRIP)
    for i in range(12):
        ext_t[:, i * 128 : (i + 1) * 128] = ext[i * 128 : (i + 1) * 128].T
    fill_mask(mask)

    def tile(step, carry):
        strip, half = 1 + (step & 1), step >> 1
        starts = slab_starts(strip - 1, half)
        _, pair = query_pair(kvqg_ref[half * 4 + strip, 1])
        keys = jnp.concatenate([ext[pl.ds(s, 256), :] for s in starts], 0)
        score = dot(keys, pair[:TOK], NT) + (mask[...] + edge_bias(place_ref, strip, half))
        top = jnp.max(score, 0, keepdims=True)
        terms = jnp.exp(score - top)
        stat_ref[step] = jnp.concatenate([top, jnp.sum(terms, 0, keepdims=True)], 0)
        slabs_t = jnp.concatenate([ext_t[HD:, pl.ds(s, 256)] for s in starts], 1)
        near_ref[step] = dot(slabs_t, terms.astype(BF))
        return carry

    lax.fori_loop(0, 4, tile, 0, unroll=2)


def forward_kernel(
    place_ref, kvqg_ref, top_ref, bottom_ref, left_ref, right_ref, marks_ref, near_ref, near_stat_ref,
    part_ref, stat_ref, dmark_ref,
    ext, ext_t, mask, dmark,
):
    fill_region(kvqg_ref, top_ref, bottom_ref, left_ref, right_ref, ext, ext_t)
    kv_mark = rows_of(marks_ref, 0).astype(BF)
    kv_mark_t = jnp.concatenate([kv_mark[0:128].T, kv_mark[128:256].T], 1)
    fill_mask(mask)
    dmark[...] = jnp.zeros_like(dmark)

    def whole_tile(step, carry):
        strip, half = 3 * (step & 1), step >> 1
        index = half * 4 + strip
        starts = slab_starts(strip, half)
        wide, pair = query_pair(kvqg_ref[index, 1])
        near_keys = jnp.concatenate([ext[pl.ds(s, 256), :] for s in starts], 0)
        near_score = dot(near_keys, pair[:TOK], NT) + (mask[...] + edge_bias(place_ref, strip, half))
        both = dot(kv_mark, pair, NT)
        mark_score, mark_inner = both[:, :TOK], both[:, TOK:]
        top = jnp.maximum(
            jnp.max(near_score, 0, keepdims=True), jnp.max(mark_score, 0, keepdims=True)
        )
        near_terms, mark_terms = jnp.exp(near_score - top), jnp.exp(mark_score - top)
        total = jnp.sum(near_terms, 0, keepdims=True) + jnp.sum(mark_terms, 0, keepdims=True)
        share = 1.0 / total
        prob = mark_terms * share
        weights = prob.astype(BF)
        near_weights = (near_terms * share).astype(BF)
        slabs_t = jnp.concatenate([ext_t[HD:, pl.ds(s, 256)] for s in starts] + [kv_mark_t[HD:]], 1)
        mixed = dot(slabs_t, jnp.concatenate([near_weights, weights], 0))
        delta = jnp.sum(wide.T[HD:] * mixed, 0, keepdims=True)
        dscore = (prob * (mark_inner - delta)).astype(BF)
        part_ref[index] = jnp.concatenate([mixed, dot(kv_mark_t[:HD], dscore)], 0).astype(BF)
        stat_ref[index] = jnp.concatenate([top + jnp.log(total), delta], 0)
        dmark[...] += dot(jnp.concatenate([dscore, weights], 1), pair)
        return carry

    def mark_tile(step, carry):
        index = (step >> 1) * 4 + 1 + (step & 1)
        wide, pair = query_pair(kvqg_ref[index, 1])
        both = dot(kv_mark, pair, NT)
        score, inner = both[:, :TOK], both[:, TOK:]
        near_top, near_total = near_stat_ref[step, 0:1], near_stat_ref[step, 1:2]
        top = jnp.maximum(near_top, jnp.max(score, 0, keepdims=True))
        terms = jnp.exp(score - top)
        near_factor = jnp.exp(near_top - top)
        total = near_factor * near_total + jnp.sum(terms, 0, keepdims=True)
        share = 1.0 / total
        prob = terms * share
        weights = prob.astype(BF)
        mixed = dot(kv_mark_t[HD:], weights) + near_ref[step] * (near_factor * share)
        delta = jnp.sum(wide.T[HD:] * mixed, 0, keepdims=True)
        dscore = (prob * (inner - delta)).astype(BF)
        part_ref[index] = jnp.concatenate([mixed, dot(kv_mark_t[:HD], dscore)], 0).astype(BF)
        stat_ref[index] = jnp.concatenate([top + jnp.log(total), delta], 0)
        dmark[...] += dot(jnp.concatenate([dscore, weights], 1), pair)
        return carry

    lax.fori_loop(0, 4, whole_tile, 0, unroll=2)
    lax.fori_loop(0, 4, mark_tile, 0, unroll=2)
    for j in range(4):
        dmark_ref[pl.ds(j, 64, stride=4), :] = dmark[64 * j : 64 * j + 64]


def window_kernel(
    place_ref, kvqg_ref, top_ref, bottom_ref, left_ref, right_ref, part_ref, stat_ref,
    out_ref, dkv_ref, side_ref,
    ext, ext_t, mask,
):
    fill_region(kvqg_ref, top_ref, bottom_ref, left_ref, right_ref, ext, ext_t)
    fill_mask(mask)
    dkv_ref[...] = jnp.zeros_like(dkv_ref)

    def tile(index, carry):
        strip, half = index & 3, index >> 2
        starts = slab_starts(strip, half)
        _, pair = query_pair(kvqg_ref[index, 1])
        stats = stat_ref[index]
        both = dot(jnp.concatenate([ext[pl.ds(s, 256), :] for s in starts], 0), pair, NT)
        score = both[:, :TOK] + (mask[...] + edge_bias(place_ref, strip, half))
        prob = jnp.exp(score - stats[0:1])
        dscore = (prob * (both[:, TOK:] - stats[1:2])).astype(BF)
        slabs_t = jnp.concatenate([ext_t[:HD, pl.ds(s, 256)] for s in starts], 1)
        part = part_ref[index].astype(F32)
        dquery = (dot(slabs_t, dscore) + part[HD:]) * SCALE
        out_ref[index] = jnp.concatenate([part[:HD], dquery], 0).T.astype(BF)
        dkv = dot(jnp.concatenate([dscore, prob.astype(BF)], 1), pair)
        for j, s in enumerate(starts):
            dkv_ref[pl.ds(s, 256), :] += dkv[256 * j : 256 * j + 256]
        return carry

    lax.fori_loop(0, 8, tile, 0, unroll=2)
    side_ref[0] = dkv_ref[0:STRIP].astype(BF)
    side_ref[1] = dkv_ref[5 * STRIP : 6 * STRIP].astype(BF)


def land_grad_kernel(kvqg_ref, w_ref, marks_ref, grads_ref, out_ref, proj_ref):
    kv = kvqg_ref[:, 0].reshape(HEADS * TOK, 2 * HD)
    weight = w_ref[...]
    log_total = rows_of(marks_ref, 4)[:, :1]
    grads = rows_of(grads_ref, 0)
    column = rows_of(grads_ref, 4)[:, :1]
    prob = jnp.exp(dot(weight, kv, NT) - log_total)
    hi, lo = split_hi_lo(grads)
    dprob = dot(hi, kv, NT) + dot(lo, kv, NT)
    dlogit = prob * (dprob - column)
    dlogit_bf, dlogit_lo = split_hi_lo(dlogit)
    prob_bf, prob_lo = split_hi_lo(prob)
    flip = lambda a: jnp.concatenate([a[:128].T, a[128:].T], 1)
    hi_t, lo_t, weight_t = flip(hi), flip(lo), flip(weight)
    left_t = jnp.concatenate([hi_t, weight_t, hi_t, weight_t, lo_t], 1)
    right = jnp.concatenate([prob_bf, dlogit_bf, prob_lo, dlogit_lo, prob_bf], 0)
    land = dot(left_t, right)
    for i in range(HEADS):
        out_ref[i] = land[:, i * TOK : (i + 1) * TOK].T
    proj = dot(dlogit_bf, kv) + dot(dlogit_lo, kv)
    proj = jnp.concatenate([proj[128 * i : 128 * i + 128].T[:HD] for i in range(2)], 0)
    proj_ref[...] = jnp.broadcast_to(proj.astype(BF)[None], proj_ref.shape)


def shape(dims, dtype=F32):
    return jax.ShapeDtypeStruct(dims, dtype)


def swap(x, axes):
    return lax.all_to_all(x, axes, 0, 0, tiled=True)


def shift(x, axis, step):
    n = lax.axis_size(axis)
    return lax.ppermute(x, axis, [(i, i + step) for i in range(n) if 0 <= i + step < n])


def per_device(query_feats, key_feats, value_feats, proj_weight, cotangent):
    rows, cols, feats = query_feats.shape
    flat = lambda a: a.reshape(TOK, feats)
    head = lax.axis_index("core") * lax.axis_size("x") + lax.axis_index("x")
    weight = lax.dynamic_index_in_dim(proj_weight, head, 0, keepdims=False)
    weight = jnp.pad(weight.T, ((0, 0), (0, HD)))
    place = jnp.stack(
        [lax.axis_index("z"), lax.axis_index("y"), lax.axis_size("z"), lax.axis_size("y")]
    ).astype(jnp.int32)

    packed = pl.pallas_call(
        pack_kernel,
        in_specs=[pl.BlockSpec(memory_space=pltpu.HBM)] * 4,
        out_shape=shape((HEADS, 2, TOK, 2 * HD), BF),
        scratch_shapes=[pltpu.VMEM((4, TOK, feats), BF), pltpu.SemaphoreType.DMA((4,))],
        compiler_params=pltpu.CompilerParams(vmem_limit_bytes=PACK_VMEM),
        cost_estimate=pl.CostEstimate(flops=0, bytes_accessed=2**20, transcendentals=0),
    )(flat(key_feats), flat(value_feats), flat(query_feats), flat(cotangent))
    own = swap(packed, GROUP)

    sums = call(sums_kernel, shape((512, 128)), flops=2 * 3 * 2**25, nbytes=2**19, trans=2**18)(own, weight)

    top = shift(own[4:8, 0, 64:], "z", 1)
    bottom = shift(own[0:4, 0, :64], "z", -1)
    strip_of = lambda x: jnp.concatenate([top[x], own[x, 0], own[4 + x, 0], bottom[x]], 0)
    left = shift(strip_of(3), "y", 1)
    right = shift(strip_of(0), "y", -1)

    means, mean = call(means_kernel, (shape((64, 8, 128)), shape((8, 128))), nbytes=2**19)(
        swap(sums.reshape(64, 8, 128), BLOCKS)
    )
    marks = swap(means, BLOCKS).reshape(512, 128)

    smem, vmem = pl.BlockSpec(memory_space=pltpu.SMEM), pl.BlockSpec(memory_space=pltpu.VMEM)
    region = [
        pltpu.VMEM((6 * STRIP, 2 * HD), BF),
        pltpu.VMEM((2 * HD, 6 * STRIP), BF),
        pltpu.VMEM((768, TOK), F32),
    ]
    near, near_stats = pl.pallas_call(
        near_kernel,
        in_specs=[smem] + [vmem] * 3,
        out_shape=(shape((4, HD, TOK)), shape((4, 2, TOK))),
        scratch_shapes=[
            pltpu.VMEM((4 * STRIP, 2 * HD), BF),
            pltpu.VMEM((2 * HD, 4 * STRIP), BF),
            pltpu.VMEM((768, TOK), F32),
        ],
        compiler_params=pltpu.CompilerParams(vmem_limit_bytes=VMEM),
        cost_estimate=pl.CostEstimate(flops=2**31, bytes_accessed=2**22, transcendentals=2**20),
    )(place, own, top, bottom)
    part, stats, dmark = pl.pallas_call(
        forward_kernel,
        in_specs=[smem] + [vmem] * 8,
        out_shape=(
            shape((HEADS, 2 * HD, TOK), BF),
            shape((HEADS, 2, TOK)),
            shape((LAND, 2 * HD)),
        ),
        scratch_shapes=region + [pltpu.VMEM((LAND, 2 * HD), F32)],
        compiler_params=pltpu.CompilerParams(vmem_limit_bytes=VMEM),
        cost_estimate=pl.CostEstimate(flops=2**31, bytes_accessed=2**22, transcendentals=2**20),
    )(place, own, top, bottom, left, right, marks, near, near_stats)

    out_q, dkv, sides = pl.pallas_call(
        window_kernel,
        in_specs=[smem] + [vmem] * 7,
        out_shape=(
            shape((HEADS, TOK, 2 * HD), BF),
            shape((6 * STRIP, 2 * HD)),
            shape((2, STRIP, 2 * HD), BF),
        ),
        scratch_shapes=region,
        compiler_params=pltpu.CompilerParams(vmem_limit_bytes=VMEM),
        cost_estimate=pl.CostEstimate(flops=2**32, bytes_accessed=2**22, transcendentals=2**20),
    )(place, own, top, bottom, left, right, part, stats)
    from_right = shift(sides[0], "y", -1)
    from_left = shift(sides[1], "y", 1)
    to_above, to_below = call(edge_kernel, (shape((4, 64, 2 * HD), BF),) * 2, nbytes=2**18)(
        dkv, from_left, from_right
    )
    from_below = shift(to_above, "z", -1)
    from_above = shift(to_below, "z", 1)

    grads = call(land_sum_kernel, shape((64, 8, 128)), nbytes=2**19, after=(sides,))(
        swap(dmark.reshape(64, 4, 128), BLOCKS).reshape(256, 128), mean
    )
    grads = swap(grads, BLOCKS).reshape(512, 128)

    land, proj = call(
        land_grad_kernel,
        (shape((HEADS, TOK, 2 * HD)), shape((8, 128, 128), BF)),
        flops=2 * 8 * 2**25, nbytes=2**20, trans=2**18, after=(to_above, to_below),
    )(own, weight, marks, grads)
    proj = swap(call(proj_sum_kernel, shape((8, 128, 128), BF))(swap(proj, "z")), "y")
    final = call(final_pack_kernel, shape((HEADS, 3, TOK, 128), BF), nbytes=2**20)(
        out_q, land, dkv, from_left, from_right, from_above, from_below, proj
    )
    *tokens, grad_proj = call(
        unpack_kernel,
        (shape((TOK, feats), BF),) * 4 + (shape((HEADS, HD, LAND)),),
        nbytes=2**20,
    )(swap(final, GROUP))
    return *(a.reshape(rows, cols, feats) for a in tokens), grad_proj


def solution(mesh):
    total_rows, total_cols = mesh.devices.shape
    fine = Mesh(mesh.devices.reshape(total_rows // 2, 2, total_cols // 4, 4), ("z", "core", "y", "x"))
    tokens = P(("z", "core"), ("y", "x"), None)
    return jax.shard_map(
        per_device,
        mesh=fine,
        in_specs=(tokens, tokens, tokens, P(), tokens),
        out_specs=(tokens, tokens, tokens, tokens, P()),
        check_vma=False,
    )
```

```python
import jax
import jax.numpy as jnp
from jax import lax
from jax.experimental import pallas as pl
from jax.experimental.pallas import tpu as pltpu
from jax.sharding import Mesh, PartitionSpec as P

RAD = 8
HEADS = 8
HD = 64
LAND = 256
TOK = 128
STRIP = 384
SCALE = HD**-0.5
NEG = -1e30
VMEM = 24 * 2**20
PACK_VMEM = 2**26 - 2**18
BF = jnp.bfloat16
F32 = jnp.float32
GROUP = ("core", "x")
BLOCKS = ("z", "y")
NT = (((1,), (1,)), ((), ()))


def call(body, outs, flops=0, nbytes=0, trans=0, after=()):
    def ordered(*refs):
        return body(*refs[len(after) :])

    return lambda *args: pl.pallas_call(
        ordered,
        out_shape=outs,
        in_specs=[pl.BlockSpec(memory_space=pl.ANY)] * len(after)
        + [pl.BlockSpec(memory_space=pltpu.VMEM)] * len(args),
        compiler_params=pltpu.CompilerParams(vmem_limit_bytes=VMEM),
        cost_estimate=pl.CostEstimate(flops=flops, bytes_accessed=nbytes, transcendentals=trans),
    )(*after, *args)


def dot(a, b, dims=(((1,), (0,)), ((), ()))):
    return lax.dot_general(a, b, dims, preferred_element_type=F32)


def split_hi_lo(x):
    hi = x.astype(BF)
    return hi, (x - hi.astype(F32)).astype(BF)


def pack_kernel(k_hbm, v_hbm, q_hbm, g_hbm, out_ref, held, sems):
    copies = [
        pltpu.make_async_copy(source, held.at[i], sems.at[i])
        for i, source in enumerate((k_hbm, v_hbm, q_hbm, g_hbm))
    ]
    for copy in copies:
        copy.start()
    for copy in copies:
        copy.wait()
    for h in range(HEADS):
        at = slice(h * HD, (h + 1) * HD)
        for part in range(2):
            out_ref[h, part] = jnp.concatenate([held[2 * part, :, at], held[2 * part + 1, :, at]], 1)


def final_pack_kernel(out_q_ref, land_ref, dkv_ref, left_ref, right_ref, above_ref, below_ref, proj_ref, out_ref):
    proj = sum_of_eight(proj_ref)
    for h in range(HEADS):
        half, strip = h // 4, h % 4
        base = (strip + 1) * STRIP + 64 + half * TOK
        grads = land_ref[h] + dkv_ref[base : base + TOK]
        if strip == 0:
            grads += left_ref[64 + half * TOK : 64 + half * TOK + TOK].astype(F32)
        if strip == 3:
            grads += right_ref[64 + half * TOK : 64 + half * TOK + TOK].astype(F32)
        zero = jnp.zeros((64, 2 * HD), F32)
        if half == 0:
            grads += jnp.concatenate([above_ref[strip].astype(F32), zero], 0)
        else:
            grads += jnp.concatenate([zero, below_ref[strip].astype(F32)], 0)
        out_ref[h, 0] = out_q_ref[h]
        out_ref[h, 1] = grads.astype(BF)
        out_ref[h, 2] = proj


def edge_kernel(dkv_ref, left_ref, right_ref, top_ref, bottom_ref):
    for strip in range(4):
        base = (strip + 1) * STRIP
        for ref, first in ((top_ref, 0), (bottom_ref, 320)):
            grads = dkv_ref[base + first : base + first + 64]
            if strip == 0:
                grads += left_ref[first : first + 64].astype(F32)
            if strip == 3:
                grads += right_ref[first : first + 64].astype(F32)
            ref[strip] = grads.astype(BF)


def unpack_kernel(in_ref, att_ref, dq_ref, dk_ref, dv_ref, proj_ref):
    for i in range(HEADS // 2):
        at = slice(i * 2 * HD, (i + 1) * 2 * HD)
        for part, first_ref, second_ref in ((0, att_ref, dq_ref), (1, dk_ref, dv_ref)):
            even, odd = in_ref[2 * i, part], in_ref[2 * i + 1, part]
            first_ref[:, at] = jnp.concatenate([even[:, :HD], odd[:, :HD]], 1)
            second_ref[:, at] = jnp.concatenate([even[:, HD:], odd[:, HD:]], 1)
    for h in range(HEADS):
        proj_ref[h, :, :128] = in_ref[h, 2, :HD].astype(F32)
        proj_ref[h, :, 128:] = in_ref[h, 2, HD:].astype(F32)


def sums_kernel(kvqg_ref, w_ref, out_ref):
    kv = kvqg_ref[:, 0].reshape(HEADS * TOK, 2 * HD)
    logits = dot(w_ref[...], kv, NT)
    top = jnp.max(logits, 1, keepdims=True)
    terms = jnp.exp(logits - top)
    total = jnp.sum(terms, 1, keepdims=True)
    hi, lo = split_hi_lo(terms)
    sums = dot(hi, kv) + dot(lo, kv)
    lane = lax.broadcasted_iota(jnp.int32, (LAND, 2 * HD), 1)
    stats = jnp.where(lane < HD, top, total)
    for j in range(4):
        out_ref[pl.ds(j, 64, stride=8), :] = sums[64 * j : 64 * j + 64]
        out_ref[pl.ds(4 + j, 64, stride=8), :] = stats[64 * j : 64 * j + 64]


def means_kernel(in_ref, out_ref):
    got = in_ref[...]
    stats = pltpu.roll(got, 4, 1)
    other = pltpu.roll(stats, HD, 2)
    low = lax.broadcasted_iota(jnp.int32, got.shape, 2) < HD
    tops = jnp.where(low, stats, other)
    totals = jnp.where(low, other, stats)
    top = jnp.max(tops, 0, keepdims=True)
    factor = jnp.exp(tops - top)
    total = jnp.sum(factor * totals, 0)
    mean = jnp.sum(factor * got, 0) / total
    log_total = top[0] + jnp.log(total)
    row = lax.broadcasted_iota(jnp.int32, mean.shape, 0)
    result = jnp.where(row < 4, mean, pltpu.roll(log_total, 4, 0))
    out_ref[...] = jnp.broadcast_to(result[None], out_ref.shape)


def land_sum_kernel(in_ref, out_ref):
    grads = jnp.sum(in_ref[...].reshape(32, 8, 2 * HD), 0)
    grads = grads + pltpu.roll(grads, 4, 0)
    out_ref[...] = jnp.broadcast_to(grads[None], (32, 8, 2 * HD)).reshape(out_ref.shape)


def sum_of_eight(in_ref):
    total = in_ref[0].astype(F32)
    for i in range(1, 8):
        total += in_ref[i].astype(F32)
    return total.astype(BF)


def proj_sum_kernel(in_ref, out_ref):
    out_ref[...] = jnp.broadcast_to(sum_of_eight(in_ref)[None], out_ref.shape)


def rows_of(ref, first, stride=8):
    return jnp.concatenate([ref[pl.ds(first + j, 64, stride=stride), :] for j in range(4)], 0)


def fill_mask(mask):
    key = lax.broadcasted_iota(jnp.int32, (768, TOK), 0)
    query = lax.broadcasted_iota(jnp.int32, (768, TOK), 1)
    row_gap = ((key >> 3) & 31) - 8 - (query >> 3)
    col_gap = ((key >> 8) - 1) * 8 + (key & 7) - (query & 7)
    near = (row_gap >= -RAD) & (row_gap <= RAD) & (col_gap >= -RAD) & (col_gap <= RAD)
    mask[...] = jnp.where(near, 0.0, NEG)


def edge_bias(place_ref, strip, half):
    column = lax.broadcasted_iota(jnp.int32, (768, 1), 0)
    key_row, key_slab = (column >> 3) & 31, column >> 8
    low_row = jnp.where((place_ref[0] == 0) & (half == 0), 8, 0)
    high_row = jnp.where((place_ref[0] == place_ref[2] - 1) & (half == 1), 24, 32)
    low_slab = jnp.where((place_ref[1] == 0) & (strip == 0), 1, 0)
    high_slab = jnp.where((place_ref[1] == place_ref[3] - 1) & (strip == 3), 1, 2)
    inside = (key_row >= low_row) & (key_row < high_row) & (key_slab >= low_slab) & (key_slab <= high_slab)
    return jnp.where(inside, 0.0, NEG)


def query_pair(query_grad):
    lane = lax.broadcasted_iota(jnp.int32, (TOK, 2 * HD), 1)
    wide = query_grad.astype(F32)
    upper = jnp.where(lane < HD, wide * SCALE, 0.0).astype(BF)
    lower = jnp.where(lane < HD, 0.0, wide).astype(BF)
    return wide, jnp.concatenate([upper, lower], 0)


def slab_starts(strip, half):
    return [pl.multiple_of((strip + j) * STRIP + half * TOK, 128) for j in range(3)]


def fill_strip(kvqg_ref, top_ref, bottom_ref, ext, x, base):
    ext[base : base + 64] = top_ref[x]
    ext[base + 64 : base + 192] = kvqg_ref[x, 0]
    ext[base + 192 : base + 320] = kvqg_ref[4 + x, 0]
    ext[base + 320 : base + 384] = bottom_ref[x]


def fill_region(kvqg_ref, top_ref, bottom_ref, left_ref, right_ref, ext):
    for x in range(4):
        fill_strip(kvqg_ref, top_ref, bottom_ref, ext, x, (x + 1) * STRIP)
    ext[0:STRIP] = left_ref[...]
    ext[5 * STRIP : 6 * STRIP] = right_ref[...]


def near_kernel(place_ref, kvqg_ref, top_ref, bottom_ref, near_ref, stat_ref, ext_t, mask, ext):
    for x in range(4):
        fill_strip(kvqg_ref, top_ref, bottom_ref, ext, x, x * STRIP)
    for i in range(12):
        ext_t[:, i * 128 : (i + 1) * 128] = ext[i * 128 : (i + 1) * 128].T
    fill_mask(mask)

    def tile(step, carry):
        strip, half = 1 + (step & 1), step >> 1
        starts = slab_starts(strip - 1, half)
        _, pair = query_pair(kvqg_ref[half * 4 + strip, 1])
        keys = jnp.concatenate([ext[pl.ds(s, 256), :] for s in starts], 0)
        score = dot(keys, pair[:TOK], NT) + (mask[...] + edge_bias(place_ref, strip, half))
        top = jnp.max(score, 0, keepdims=True)
        terms = jnp.exp(score - top)
        stat_ref[step] = jnp.concatenate([top, jnp.sum(terms, 0, keepdims=True)], 0)
        slabs_t = jnp.concatenate([ext_t[HD:, pl.ds(s, 256)] for s in starts], 1)
        near_ref[step] = dot(slabs_t, terms.astype(BF))
        return carry

    lax.fori_loop(0, 4, tile, 0, unroll=2)


def forward_kernel(
    place_ref, kvqg_ref, top_ref, bottom_ref, left_ref, right_ref, marks_ref,
    near_ref, near_stat_ref, own_t_ref, mask,
    part_ref, stat_ref, dmark_ref,
    ext, ext_t, dmark,
):
    fill_region(kvqg_ref, top_ref, bottom_ref, left_ref, right_ref, ext)
    ext_t[:, STRIP : 5 * STRIP] = own_t_ref[...]
    for i in (0, 1, 2, 15, 16, 17):
        ext_t[:, i * 128 : (i + 1) * 128] = ext[i * 128 : (i + 1) * 128].T
    kv_mark = rows_of(marks_ref, 0).astype(BF)
    kv_mark_t = jnp.concatenate([kv_mark[0:128].T, kv_mark[128:256].T], 1)
    dmark[...] = jnp.zeros_like(dmark)

    def whole_tile(step, carry):
        strip, half = 3 * (step & 1), step >> 1
        index = half * 4 + strip
        starts = slab_starts(strip, half)
        wide, pair = query_pair(kvqg_ref[index, 1])
        near_keys = jnp.concatenate([ext[pl.ds(s, 256), :] for s in starts], 0)
        near_score = dot(near_keys, pair[:TOK], NT) + (mask[...] + edge_bias(place_ref, strip, half))
        both = dot(kv_mark, pair, NT)
        mark_score, mark_inner = both[:, :TOK], both[:, TOK:]
        top = jnp.maximum(
            jnp.max(near_score, 0, keepdims=True), jnp.max(mark_score, 0, keepdims=True)
        )
        near_terms, mark_terms = jnp.exp(near_score - top), jnp.exp(mark_score - top)
        total = jnp.sum(near_terms, 0, keepdims=True) + jnp.sum(mark_terms, 0, keepdims=True)
        share = 1.0 / total
        prob = mark_terms * share
        weights = prob.astype(BF)
        near_weights = (near_terms * share).astype(BF)
        slabs_t = jnp.concatenate([ext_t[HD:, pl.ds(s, 256)] for s in starts] + [kv_mark_t[HD:]], 1)
        mixed = dot(slabs_t, jnp.concatenate([near_weights, weights], 0))
        delta = jnp.sum(wide.T[HD:] * mixed, 0, keepdims=True)
        dscore = (prob * (mark_inner - delta)).astype(BF)
        part_ref[index] = jnp.concatenate([mixed, dot(kv_mark_t[:HD], dscore)], 0).astype(BF)
        stat_ref[index] = jnp.concatenate([top + jnp.log(total), delta], 0)
        dmark[...] += dot(jnp.concatenate([dscore, weights], 1), pair)
        return carry

    def mark_tile(step, carry):
        index = (step >> 1) * 4 + 1 + (step & 1)
        wide, pair = query_pair(kvqg_ref[index, 1])
        both = dot(kv_mark, pair, NT)
        score, inner = both[:, :TOK], both[:, TOK:]
        near_top, near_total = near_stat_ref[step, 0:1], near_stat_ref[step, 1:2]
        top = jnp.maximum(near_top, jnp.max(score, 0, keepdims=True))
        terms = jnp.exp(score - top)
        near_factor = jnp.exp(near_top - top)
        total = near_factor * near_total + jnp.sum(terms, 0, keepdims=True)
        share = 1.0 / total
        prob = terms * share
        weights = prob.astype(BF)
        mixed = dot(kv_mark_t[HD:], weights) + near_ref[step] * (near_factor * share)
        delta = jnp.sum(wide.T[HD:] * mixed, 0, keepdims=True)
        dscore = (prob * (inner - delta)).astype(BF)
        part_ref[index] = jnp.concatenate([mixed, dot(kv_mark_t[:HD], dscore)], 0).astype(BF)
        stat_ref[index] = jnp.concatenate([top + jnp.log(total), delta], 0)
        dmark[...] += dot(jnp.concatenate([dscore, weights], 1), pair)
        return carry

    lax.fori_loop(0, 4, whole_tile, 0, unroll=2)
    lax.fori_loop(0, 4, mark_tile, 0, unroll=2)
    for j in range(4):
        dmark_ref[pl.ds(j, 64, stride=4), :] = dmark[64 * j : 64 * j + 64]


def window_kernel(
    place_ref, kvqg_ref, top_ref, bottom_ref, left_ref, right_ref, part_ref, stat_ref,
    out_ref, dkv_ref,
    ext, ext_t, mask,
):
    fill_region(kvqg_ref, top_ref, bottom_ref, left_ref, right_ref, ext)
    for i in range(18):
        ext_t[:, i * 128 : (i + 1) * 128] = ext[i * 128 : (i + 1) * 128].T
    fill_mask(mask)
    dkv_ref[...] = jnp.zeros_like(dkv_ref)

    def tile(index, carry):
        strip, half = index & 3, index >> 2
        starts = slab_starts(strip, half)
        _, pair = query_pair(kvqg_ref[index, 1])
        stats = stat_ref[index]
        both = dot(jnp.concatenate([ext[pl.ds(s, 256), :] for s in starts], 0), pair, NT)
        score = both[:, :TOK] + (mask[...] + edge_bias(place_ref, strip, half))
        prob = jnp.exp(score - stats[0:1])
        dscore = (prob * (both[:, TOK:] - stats[1:2])).astype(BF)
        slabs_t = jnp.concatenate([ext_t[:HD, pl.ds(s, 256)] for s in starts], 1)
        part = part_ref[index].astype(F32)
        dquery = (dot(slabs_t, dscore) + part[HD:]) * SCALE
        out_ref[index] = jnp.concatenate([part[:HD], dquery], 0).T.astype(BF)
        dkv = dot(jnp.concatenate([dscore, prob.astype(BF)], 1), pair)
        for j, s in enumerate(starts):
            dkv_ref[pl.ds(s, 256), :] += dkv[256 * j : 256 * j + 256]
        return carry

    lax.fori_loop(0, 8, tile, 0, unroll=2)


def land_grad_kernel(kvqg_ref, w_ref, marks_ref, grads_ref, dkv_ref, out_ref, proj_ref, side_ref):
    side_ref[0] = dkv_ref[0:STRIP].astype(BF)
    side_ref[1] = dkv_ref[5 * STRIP : 6 * STRIP].astype(BF)
    kv = kvqg_ref[:, 0].reshape(HEADS * TOK, 2 * HD)
    weight = w_ref[...]
    log_total = rows_of(marks_ref, 4)[:, :1]
    grads = rows_of(grads_ref, 0, 4)
    column = jnp.sum(rows_of(marks_ref, 0) * grads, 1, keepdims=True)
    prob = jnp.exp(dot(weight, kv, NT) - log_total)
    hi, lo = split_hi_lo(grads)
    dprob = dot(hi, kv, NT) + dot(lo, kv, NT)
    dlogit = prob * (dprob - column)
    dlogit_bf, dlogit_lo = split_hi_lo(dlogit)
    prob_bf, prob_lo = split_hi_lo(prob)
    flip = lambda a: jnp.concatenate([a[:128].T, a[128:].T], 1)
    hi_t, lo_t, weight_t = flip(hi), flip(lo), flip(weight)
    left_t = jnp.concatenate([hi_t, weight_t, hi_t, weight_t, lo_t], 1)
    right = jnp.concatenate([prob_bf, dlogit_bf, prob_lo, dlogit_lo, prob_bf], 0)
    land = dot(left_t, right)
    for i in range(HEADS):
        out_ref[i] = land[:, i * TOK : (i + 1) * TOK].T
    proj = dot(dlogit_bf, kv) + dot(dlogit_lo, kv)
    proj = jnp.concatenate([proj[128 * i : 128 * i + 128].T[:HD] for i in range(2)], 0)
    proj_ref[...] = jnp.broadcast_to(proj.astype(BF)[None], proj_ref.shape)


def shape(dims, dtype=F32):
    return jax.ShapeDtypeStruct(dims, dtype)


def swap(x, axes):
    return lax.all_to_all(x, axes, 0, 0, tiled=True)


def shift(x, axis, step):
    n = lax.axis_size(axis)
    return lax.ppermute(x, axis, [(i, i + step) for i in range(n) if 0 <= i + step < n])


def per_device(query_feats, key_feats, value_feats, proj_weight, cotangent):
    rows, cols, feats = query_feats.shape
    flat = lambda a: a.reshape(TOK, feats)
    head = lax.axis_index("core") * lax.axis_size("x") + lax.axis_index("x")
    weight = lax.dynamic_index_in_dim(proj_weight, head, 0, keepdims=False)
    weight = jnp.pad(weight.T, ((0, 0), (0, HD)))
    place = jnp.stack(
        [lax.axis_index("z"), lax.axis_index("y"), lax.axis_size("z"), lax.axis_size("y")]
    ).astype(jnp.int32)

    packed = pl.pallas_call(
        pack_kernel,
        in_specs=[pl.BlockSpec(memory_space=pltpu.HBM)] * 4,
        out_shape=shape((HEADS, 2, TOK, 2 * HD), BF),
        scratch_shapes=[pltpu.VMEM((4, TOK, feats), BF), pltpu.SemaphoreType.DMA((4,))],
        compiler_params=pltpu.CompilerParams(vmem_limit_bytes=PACK_VMEM),
        cost_estimate=pl.CostEstimate(flops=0, bytes_accessed=2**20, transcendentals=0),
    )(flat(key_feats), flat(value_feats), flat(query_feats), flat(cotangent))
    own = swap(packed, GROUP)

    sums = call(sums_kernel, shape((512, 128)), flops=2 * 3 * 2**25, nbytes=2**19, trans=2**18)(own, weight)

    top = shift(own[4:8, 0, 64:], "z", 1)
    bottom = shift(own[0:4, 0, :64], "z", -1)
    strip_of = lambda x: jnp.concatenate([top[x], own[x, 0], own[4 + x, 0], bottom[x]], 0)
    left = shift(strip_of(3), "y", 1)
    right = shift(strip_of(0), "y", -1)

    means = call(means_kernel, shape((64, 8, 128)), nbytes=2**19)(swap(sums.reshape(64, 8, 128), BLOCKS))
    marks = swap(means, BLOCKS).reshape(512, 128)

    smem, vmem = pl.BlockSpec(memory_space=pltpu.SMEM), pl.BlockSpec(memory_space=pltpu.VMEM)
    region = [
        pltpu.VMEM((6 * STRIP, 2 * HD), BF),
        pltpu.VMEM((2 * HD, 6 * STRIP), BF),
        pltpu.VMEM((768, TOK), F32),
    ]
    near = pl.pallas_call(
        near_kernel,
        in_specs=[smem] + [vmem] * 3,
        out_shape=(
            shape((4, HD, TOK)),
            shape((4, 2, TOK)),
            shape((2 * HD, 4 * STRIP), BF),
            shape((768, TOK)),
        ),
        scratch_shapes=[pltpu.VMEM((4 * STRIP, 2 * HD), BF)],
        compiler_params=pltpu.CompilerParams(vmem_limit_bytes=VMEM),
        cost_estimate=pl.CostEstimate(flops=2**31, bytes_accessed=2**22, transcendentals=2**20),
    )(place, own, top, bottom)
    part, stats, dmark = pl.pallas_call(
        forward_kernel,
        in_specs=[smem] + [vmem] * 10,
        out_shape=(
            shape((HEADS, 2 * HD, TOK), BF),
            shape((HEADS, 2, TOK)),
            shape((LAND, 2 * HD)),
        ),
        scratch_shapes=region[:2] + [pltpu.VMEM((LAND, 2 * HD), F32)],
        compiler_params=pltpu.CompilerParams(vmem_limit_bytes=VMEM),
        cost_estimate=pl.CostEstimate(flops=2**31, bytes_accessed=2**22, transcendentals=2**20),
    )(place, own, top, bottom, left, right, marks, *near)

    out_q, dkv = pl.pallas_call(
        window_kernel,
        in_specs=[smem] + [vmem] * 7,
        out_shape=(
            shape((HEADS, TOK, 2 * HD), BF),
            shape((6 * STRIP, 2 * HD)),
        ),
        scratch_shapes=region,
        compiler_params=pltpu.CompilerParams(vmem_limit_bytes=VMEM),
        cost_estimate=pl.CostEstimate(flops=2**32, bytes_accessed=2**22, transcendentals=2**20),
    )(place, own, top, bottom, left, right, part, stats)
    grads = call(land_sum_kernel, shape((256, 128)), nbytes=2**18, after=(out_q,))(
        swap(dmark.reshape(64, 4, 128), BLOCKS).reshape(256, 128)
    )
    grads = swap(grads.reshape(64, 4, 128), BLOCKS).reshape(256, 128)

    land, proj, sides = call(
        land_grad_kernel,
        (shape((HEADS, TOK, 2 * HD)), shape((8, 128, 128), BF), shape((2, STRIP, 2 * HD), BF)),
        flops=2 * 8 * 2**25, nbytes=2**20, trans=2**18,
    )(own, weight, marks, grads, dkv)
    from_right = shift(sides[0], "y", -1)
    from_left = shift(sides[1], "y", 1)
    to_above, to_below = call(edge_kernel, (shape((4, 64, 2 * HD), BF),) * 2, nbytes=2**18)(
        dkv, from_left, from_right
    )
    from_below = shift(to_above, "z", -1)
    from_above = shift(to_below, "z", 1)

    proj = swap(call(proj_sum_kernel, shape((8, 128, 128), BF), after=(to_above, to_below))(swap(proj, "z")), "y")
    final = call(final_pack_kernel, shape((HEADS, 3, TOK, 128), BF), nbytes=2**20)(
        out_q, land, dkv, from_left, from_right, from_above, from_below, proj
    )
    *tokens, grad_proj = call(
        unpack_kernel,
        (shape((TOK, feats), BF),) * 4 + (shape((HEADS, HD, LAND)),),
        nbytes=2**20,
    )(swap(final, GROUP))
    return *(a.reshape(rows, cols, feats) for a in tokens), grad_proj


def solution(mesh):
    total_rows, total_cols = mesh.devices.shape
    fine = Mesh(mesh.devices.reshape(total_rows // 2, 2, total_cols // 4, 4), ("z", "core", "y", "x"))
    tokens = P(("z", "core"), ("y", "x"), None)
    return jax.shard_map(
        per_device,
        mesh=fine,
        in_specs=(tokens, tokens, tokens, P(), tokens),
        out_specs=(tokens, tokens, tokens, tokens, P()),
        check_vma=False,
    )
```

```python
import jax
import jax.numpy as jnp
from jax import lax
from jax.experimental import pallas as pl
from jax.experimental.pallas import tpu as pltpu
from jax.sharding import Mesh, PartitionSpec as P

RAD = 8
HEADS = 8
HD = 64
LAND = 256
TOK = 128
STRIP = 384
SCALE = HD**-0.5
NEG = -1e30
VMEM = 24 * 2**20
PACK_VMEM = 2**26 - 2**18
BF = jnp.bfloat16
F32 = jnp.float32
GROUP = ("core", "x")
BLOCKS = ("z", "y")
NT = (((1,), (1,)), ((), ()))


def call(body, outs, flops=0, nbytes=0, trans=0, after=()):
    def ordered(*refs):
        return body(*refs[len(after) :])

    return lambda *args: pl.pallas_call(
        ordered,
        out_shape=outs,
        in_specs=[pl.BlockSpec(memory_space=pl.ANY)] * len(after)
        + [pl.BlockSpec(memory_space=pltpu.VMEM)] * len(args),
        compiler_params=pltpu.CompilerParams(vmem_limit_bytes=VMEM),
        cost_estimate=pl.CostEstimate(flops=flops, bytes_accessed=nbytes, transcendentals=trans),
    )(*after, *args)


def dot(a, b, dims=(((1,), (0,)), ((), ()))):
    return lax.dot_general(a, b, dims, preferred_element_type=F32)


def split_hi_lo(x):
    hi = x.astype(BF)
    return hi, (x - hi.astype(F32)).astype(BF)


def pack_kernel(k_hbm, v_hbm, q_hbm, g_hbm, out_ref, held, sems):
    copies = [
        pltpu.make_async_copy(source, held.at[i], sems.at[i])
        for i, source in enumerate((k_hbm, v_hbm, q_hbm, g_hbm))
    ]
    for copy in copies:
        copy.start()
    for part in range(2):
        copies[2 * part].wait()
        copies[2 * part + 1].wait()
        for h in range(HEADS):
            at = slice(h * HD, (h + 1) * HD)
            out_ref[h, part] = jnp.concatenate([held[2 * part, :, at], held[2 * part + 1, :, at]], 1)


def final_pack_kernel(out_q_ref, land_ref, dkv_ref, left_ref, right_ref, above_ref, below_ref, proj_ref, out_ref):
    proj = sum_of_eight(proj_ref)
    for h in range(HEADS):
        half, strip = h // 4, h % 4
        base = (strip + 1) * STRIP + 64 + half * TOK
        grads = land_ref[h] + dkv_ref[base : base + TOK]
        if strip == 0:
            grads += left_ref[64 + half * TOK : 64 + half * TOK + TOK].astype(F32)
        if strip == 3:
            grads += right_ref[64 + half * TOK : 64 + half * TOK + TOK].astype(F32)
        zero = jnp.zeros((64, 2 * HD), F32)
        if half == 0:
            grads += jnp.concatenate([above_ref[strip].astype(F32), zero], 0)
        else:
            grads += jnp.concatenate([zero, below_ref[strip].astype(F32)], 0)
        out_ref[h, 0] = out_q_ref[h]
        out_ref[h, 1] = grads.astype(BF)
        out_ref[h, 2] = proj


def edge_kernel(dkv_ref, left_ref, right_ref, top_ref, bottom_ref):
    for strip in range(4):
        base = (strip + 1) * STRIP
        for ref, first in ((top_ref, 0), (bottom_ref, 320)):
            grads = dkv_ref[base + first : base + first + 64]
            if strip == 0:
                grads += left_ref[first : first + 64].astype(F32)
            if strip == 3:
                grads += right_ref[first : first + 64].astype(F32)
            ref[strip] = grads.astype(BF)


def unpack_kernel(in_ref, att_ref, dq_ref, dk_ref, dv_ref, proj_ref):
    for i in range(HEADS // 2):
        at = slice(i * 2 * HD, (i + 1) * 2 * HD)
        for part, first_ref, second_ref in ((0, att_ref, dq_ref), (1, dk_ref, dv_ref)):
            even, odd = in_ref[2 * i, part], in_ref[2 * i + 1, part]
            first_ref[:, at] = jnp.concatenate([even[:, :HD], odd[:, :HD]], 1)
            second_ref[:, at] = jnp.concatenate([even[:, HD:], odd[:, HD:]], 1)
    for h in range(HEADS):
        proj_ref[h, :, :128] = in_ref[h, 2, :HD].astype(F32)
        proj_ref[h, :, 128:] = in_ref[h, 2, HD:].astype(F32)


def sums_kernel(kvqg_ref, w_ref, out_ref):
    kv = kvqg_ref[:, 0].reshape(HEADS * TOK, 2 * HD)
    logits = dot(w_ref[...], kv, NT)
    top = jnp.max(logits, 1, keepdims=True)
    terms = jnp.exp(logits - top)
    total = jnp.sum(terms, 1, keepdims=True)
    hi, lo = split_hi_lo(terms)
    sums = dot(hi, kv) + dot(lo, kv)
    lane = lax.broadcasted_iota(jnp.int32, (LAND, 2 * HD), 1)
    stats = jnp.where(lane < HD, top, total)
    for j in range(4):
        out_ref[pl.ds(j, 64, stride=8), :] = sums[64 * j : 64 * j + 64]
        out_ref[pl.ds(4 + j, 64, stride=8), :] = stats[64 * j : 64 * j + 64]


def means_kernel(in_ref, out_ref):
    got = in_ref[...]
    stats = pltpu.roll(got, 4, 1)
    other = pltpu.roll(stats, HD, 2)
    low = lax.broadcasted_iota(jnp.int32, got.shape, 2) < HD
    tops = jnp.where(low, stats, other)
    totals = jnp.where(low, other, stats)
    top = jnp.max(tops, 0, keepdims=True)
    factor = jnp.exp(tops - top)
    total = jnp.sum(factor * totals, 0)
    mean = jnp.sum(factor * got, 0) / total
    log_total = top[0] + jnp.log(total)
    row = lax.broadcasted_iota(jnp.int32, mean.shape, 0)
    result = jnp.where(row < 4, mean, pltpu.roll(log_total, 4, 0))
    out_ref[...] = jnp.broadcast_to(result[None], out_ref.shape)


def land_sum_kernel(in_ref, out_ref):
    grads = jnp.sum(in_ref[...].reshape(32, 8, 2 * HD), 0)
    grads = grads + pltpu.roll(grads, 4, 0)
    out_ref[...] = jnp.broadcast_to(grads[None], (32, 8, 2 * HD)).reshape(out_ref.shape)


def sum_of_eight(in_ref):
    total = in_ref[0].astype(F32)
    for i in range(1, 8):
        total += in_ref[i].astype(F32)
    return total.astype(BF)


def proj_sum_kernel(in_ref, out_ref):
    out_ref[...] = jnp.broadcast_to(sum_of_eight(in_ref)[None], out_ref.shape)


def rows_of(ref, first, stride=8):
    return jnp.concatenate([ref[pl.ds(first + j, 64, stride=stride), :] for j in range(4)], 0)


def fill_mask(mask):
    key = lax.broadcasted_iota(jnp.int32, (768, TOK), 0)
    query = lax.broadcasted_iota(jnp.int32, (768, TOK), 1)
    row_gap = ((key >> 3) & 31) - 8 - (query >> 3)
    col_gap = ((key >> 8) - 1) * 8 + (key & 7) - (query & 7)
    near = (row_gap >= -RAD) & (row_gap <= RAD) & (col_gap >= -RAD) & (col_gap <= RAD)
    mask[...] = jnp.where(near, 0.0, NEG)


def edge_bias(place_ref, strip, half):
    column = lax.broadcasted_iota(jnp.int32, (768, 1), 0)
    key_row, key_slab = (column >> 3) & 31, column >> 8
    low_row = jnp.where((place_ref[0] == 0) & (half == 0), 8, 0)
    high_row = jnp.where((place_ref[0] == place_ref[2] - 1) & (half == 1), 24, 32)
    low_slab = jnp.where((place_ref[1] == 0) & (strip == 0), 1, 0)
    high_slab = jnp.where((place_ref[1] == place_ref[3] - 1) & (strip == 3), 1, 2)
    inside = (key_row >= low_row) & (key_row < high_row) & (key_slab >= low_slab) & (key_slab <= high_slab)
    return jnp.where(inside, 0.0, NEG)


def query_pair(query_grad):
    lane = lax.broadcasted_iota(jnp.int32, (TOK, 2 * HD), 1)
    wide = query_grad.astype(F32)
    upper = jnp.where(lane < HD, wide * SCALE, 0.0).astype(BF)
    lower = jnp.where(lane < HD, 0.0, wide).astype(BF)
    return wide, jnp.concatenate([upper, lower], 0)


def slab_starts(strip, half):
    return [pl.multiple_of((strip + j) * STRIP + half * TOK, 128) for j in range(3)]


def fill_strip(kvqg_ref, top_ref, bottom_ref, ext, x, base):
    ext[base : base + 64] = top_ref[x]
    ext[base + 64 : base + 192] = kvqg_ref[x, 0]
    ext[base + 192 : base + 320] = kvqg_ref[4 + x, 0]
    ext[base + 320 : base + 384] = bottom_ref[x]


def fill_region(kvqg_ref, top_ref, bottom_ref, left_ref, right_ref, ext):
    for x in range(4):
        fill_strip(kvqg_ref, top_ref, bottom_ref, ext, x, (x + 1) * STRIP)
    ext[0:STRIP] = left_ref[...]
    ext[5 * STRIP : 6 * STRIP] = right_ref[...]


def near_kernel(place_ref, kvqg_ref, top_ref, bottom_ref, near_ref, stat_ref, ext_t, mask, ext):
    for x in range(4):
        fill_strip(kvqg_ref, top_ref, bottom_ref, ext, x, x * STRIP)
    for i in range(12):
        ext_t[:, i * 128 : (i + 1) * 128] = ext[i * 128 : (i + 1) * 128].T
    fill_mask(mask)

    def tile(step, carry):
        strip, half = 1 + (step & 1), step >> 1
        starts = slab_starts(strip - 1, half)
        _, pair = query_pair(kvqg_ref[half * 4 + strip, 1])
        keys = jnp.concatenate([ext[pl.ds(s, 256), :] for s in starts], 0)
        score = dot(keys, pair[:TOK], NT) + (mask[...] + edge_bias(place_ref, strip, half))
        top = jnp.max(score, 0, keepdims=True)
        terms = jnp.exp(score - top)
        stat_ref[step] = jnp.concatenate([top, jnp.sum(terms, 0, keepdims=True)], 0)
        slabs_t = jnp.concatenate([ext_t[HD:, pl.ds(s, 256)] for s in starts], 1)
        near_ref[step] = dot(slabs_t, terms.astype(BF))
        return carry

    lax.fori_loop(0, 4, tile, 0, unroll=2)


def forward_kernel(
    place_ref, kvqg_ref, top_ref, bottom_ref, left_ref, right_ref, marks_ref,
    near_ref, near_stat_ref, own_t_ref, mask,
    part_ref, stat_ref, dmark_ref,
    ext, ext_t, dmark,
):
    fill_region(kvqg_ref, top_ref, bottom_ref, left_ref, right_ref, ext)
    ext_t[:, STRIP : 5 * STRIP] = own_t_ref[...]
    for i in (0, 1, 2, 15, 16, 17):
        ext_t[:, i * 128 : (i + 1) * 128] = ext[i * 128 : (i + 1) * 128].T
    kv_mark = rows_of(marks_ref, 0).astype(BF)
    kv_mark_t = jnp.concatenate([kv_mark[0:128].T, kv_mark[128:256].T], 1)
    dmark[...] = jnp.zeros_like(dmark)

    def whole_tile(step, carry):
        strip, half = 3 * (step & 1), step >> 1
        index = half * 4 + strip
        starts = slab_starts(strip, half)
        wide, pair = query_pair(kvqg_ref[index, 1])
        near_keys = jnp.concatenate([ext[pl.ds(s, 256), :] for s in starts], 0)
        near_score = dot(near_keys, pair[:TOK], NT) + (mask[...] + edge_bias(place_ref, strip, half))
        both = dot(kv_mark, pair, NT)
        mark_score, mark_inner = both[:, :TOK], both[:, TOK:]
        top = jnp.maximum(
            jnp.max(near_score, 0, keepdims=True), jnp.max(mark_score, 0, keepdims=True)
        )
        near_terms, mark_terms = jnp.exp(near_score - top), jnp.exp(mark_score - top)
        total = jnp.sum(near_terms, 0, keepdims=True) + jnp.sum(mark_terms, 0, keepdims=True)
        share = 1.0 / total
        prob = mark_terms * share
        weights = prob.astype(BF)
        near_weights = (near_terms * share).astype(BF)
        slabs_t = jnp.concatenate([ext_t[HD:, pl.ds(s, 256)] for s in starts] + [kv_mark_t[HD:]], 1)
        mixed = dot(slabs_t, jnp.concatenate([near_weights, weights], 0))
        delta = jnp.sum(wide.T[HD:] * mixed, 0, keepdims=True)
        dscore = (prob * (mark_inner - delta)).astype(BF)
        part_ref[index] = jnp.concatenate([mixed, dot(kv_mark_t[:HD], dscore)], 0).astype(BF)
        stat_ref[index] = jnp.concatenate([top + jnp.log(total), delta], 0)
        dmark[...] += dot(jnp.concatenate([dscore, weights], 1), pair)
        return carry

    def mark_tile(step, carry):
        index = (step >> 1) * 4 + 1 + (step & 1)
        wide, pair = query_pair(kvqg_ref[index, 1])
        both = dot(kv_mark, pair, NT)
        score, inner = both[:, :TOK], both[:, TOK:]
        near_top, near_total = near_stat_ref[step, 0:1], near_stat_ref[step, 1:2]
        top = jnp.maximum(near_top, jnp.max(score, 0, keepdims=True))
        terms = jnp.exp(score - top)
        near_factor = jnp.exp(near_top - top)
        total = near_factor * near_total + jnp.sum(terms, 0, keepdims=True)
        share = 1.0 / total
        prob = terms * share
        weights = prob.astype(BF)
        mixed = dot(kv_mark_t[HD:], weights) + near_ref[step] * (near_factor * share)
        delta = jnp.sum(wide.T[HD:] * mixed, 0, keepdims=True)
        dscore = (prob * (inner - delta)).astype(BF)
        part_ref[index] = jnp.concatenate([mixed, dot(kv_mark_t[:HD], dscore)], 0).astype(BF)
        stat_ref[index] = jnp.concatenate([top + jnp.log(total), delta], 0)
        dmark[...] += dot(jnp.concatenate([dscore, weights], 1), pair)
        return carry

    lax.fori_loop(0, 4, whole_tile, 0, unroll=2)
    lax.fori_loop(0, 4, mark_tile, 0, unroll=4)
    for j in range(4):
        dmark_ref[pl.ds(j, 64, stride=4), :] = dmark[64 * j : 64 * j + 64]


def window_kernel(
    place_ref, kvqg_ref, top_ref, bottom_ref, left_ref, right_ref, part_ref, stat_ref,
    out_ref, dkv_ref,
    ext, ext_t, mask,
):
    fill_region(kvqg_ref, top_ref, bottom_ref, left_ref, right_ref, ext)
    for i in range(18):
        ext_t[:, i * 128 : (i + 1) * 128] = ext[i * 128 : (i + 1) * 128].T
    fill_mask(mask)
    dkv_ref[...] = jnp.zeros_like(dkv_ref)

    def tile(index, carry):
        strip, half = index & 3, index >> 2
        starts = slab_starts(strip, half)
        _, pair = query_pair(kvqg_ref[index, 1])
        stats = stat_ref[index]
        both = dot(jnp.concatenate([ext[pl.ds(s, 256), :] for s in starts], 0), pair, NT)
        score = both[:, :TOK] + (mask[...] + edge_bias(place_ref, strip, half))
        prob = jnp.exp(score - stats[0:1])
        dscore = (prob * (both[:, TOK:] - stats[1:2])).astype(BF)
        slabs_t = jnp.concatenate([ext_t[:HD, pl.ds(s, 256)] for s in starts], 1)
        part = part_ref[index].astype(F32)
        dquery = (dot(slabs_t, dscore) + part[HD:]) * SCALE
        out_ref[index] = jnp.concatenate([part[:HD], dquery], 0).T.astype(BF)
        dkv = dot(jnp.concatenate([dscore, prob.astype(BF)], 1), pair)
        for j, s in enumerate(starts):
            dkv_ref[pl.ds(s, 256), :] += dkv[256 * j : 256 * j + 256]
        return carry

    lax.fori_loop(0, 8, tile, 0, unroll=2)


def land_grad_kernel(kvqg_ref, w_ref, marks_ref, grads_ref, first_ref, last_ref, out_ref, proj_ref, side_ref):
    side_ref[0] = first_ref[...].astype(BF)
    side_ref[1] = last_ref[...].astype(BF)
    kv = kvqg_ref[:, 0].reshape(HEADS * TOK, 2 * HD)
    weight = w_ref[...]
    log_total = rows_of(marks_ref, 4)[:, :1]
    grads = rows_of(grads_ref, 0, 4)
    column = jnp.sum(rows_of(marks_ref, 0) * grads, 1, keepdims=True)
    prob = jnp.exp(dot(weight, kv, NT) - log_total)
    hi, lo = split_hi_lo(grads)
    dprob = dot(hi, kv, NT) + dot(lo, kv, NT)
    dlogit = prob * (dprob - column)
    dlogit_bf, dlogit_lo = split_hi_lo(dlogit)
    prob_bf, prob_lo = split_hi_lo(prob)
    flip = lambda a: jnp.concatenate([a[:128].T, a[128:].T], 1)
    hi_t, lo_t, weight_t = flip(hi), flip(lo), flip(weight)
    left_t = jnp.concatenate([hi_t, weight_t, hi_t, weight_t, lo_t], 1)
    right = jnp.concatenate([prob_bf, dlogit_bf, prob_lo, dlogit_lo, prob_bf], 0)
    land = dot(left_t, right)
    for i in range(HEADS):
        out_ref[i] = land[:, i * TOK : (i + 1) * TOK].T
    proj = dot(dlogit_bf, kv) + dot(dlogit_lo, kv)
    proj = jnp.concatenate([proj[128 * i : 128 * i + 128].T[:HD] for i in range(2)], 0)
    proj_ref[...] = jnp.broadcast_to(proj.astype(BF)[None], proj_ref.shape)


def shape(dims, dtype=F32):
    return jax.ShapeDtypeStruct(dims, dtype)


def swap(x, axes):
    return lax.all_to_all(x, axes, 0, 0, tiled=True)


def shift(x, axis, step):
    n = lax.axis_size(axis)
    return lax.ppermute(x, axis, [(i, i + step) for i in range(n) if 0 <= i + step < n])


def per_device(query_feats, key_feats, value_feats, proj_weight, cotangent):
    rows, cols, feats = query_feats.shape
    flat = lambda a: a.reshape(TOK, feats)
    head = lax.axis_index("core") * lax.axis_size("x") + lax.axis_index("x")
    weight = lax.dynamic_index_in_dim(proj_weight, head, 0, keepdims=False)
    weight = jnp.pad(weight.T, ((0, 0), (0, HD)))
    place = jnp.stack(
        [lax.axis_index("z"), lax.axis_index("y"), lax.axis_size("z"), lax.axis_size("y")]
    ).astype(jnp.int32)

    packed = pl.pallas_call(
        pack_kernel,
        in_specs=[pl.BlockSpec(memory_space=pltpu.HBM)] * 4,
        out_shape=shape((HEADS, 2, TOK, 2 * HD), BF),
        scratch_shapes=[pltpu.VMEM((4, TOK, feats), BF), pltpu.SemaphoreType.DMA((4,))],
        compiler_params=pltpu.CompilerParams(vmem_limit_bytes=PACK_VMEM),
        cost_estimate=pl.CostEstimate(flops=0, bytes_accessed=2**20, transcendentals=0),
    )(flat(key_feats), flat(value_feats), flat(query_feats), flat(cotangent))
    own = swap(packed, GROUP)

    sums = call(sums_kernel, shape((512, 128)), flops=2 * 3 * 2**25, nbytes=2**19, trans=2**18)(own, weight)

    top = shift(own[4:8, 0, 64:], "z", 1)
    bottom = shift(own[0:4, 0, :64], "z", -1)
    strip_of = lambda x: jnp.concatenate([top[x], own[x, 0], own[4 + x, 0], bottom[x]], 0)
    left = shift(strip_of(3), "y", 1)
    right = shift(strip_of(0), "y", -1)

    means = call(means_kernel, shape((64, 8, 128)), nbytes=2**19)(swap(sums.reshape(64, 8, 128), BLOCKS))
    marks = swap(means, BLOCKS).reshape(512, 128)

    smem, vmem = pl.BlockSpec(memory_space=pltpu.SMEM), pl.BlockSpec(memory_space=pltpu.VMEM)
    region = [
        pltpu.VMEM((6 * STRIP, 2 * HD), BF),
        pltpu.VMEM((2 * HD, 6 * STRIP), BF),
        pltpu.VMEM((768, TOK), F32),
    ]
    near = pl.pallas_call(
        near_kernel,
        in_specs=[smem] + [vmem] * 3,
        out_shape=(
            shape((4, HD, TOK)),
            shape((4, 2, TOK)),
            shape((2 * HD, 4 * STRIP), BF),
            shape((768, TOK)),
        ),
        scratch_shapes=[pltpu.VMEM((4 * STRIP, 2 * HD), BF)],
        compiler_params=pltpu.CompilerParams(vmem_limit_bytes=VMEM),
        cost_estimate=pl.CostEstimate(flops=2**31, bytes_accessed=2**22, transcendentals=2**20),
    )(place, own, top, bottom)
    part, stats, dmark = pl.pallas_call(
        forward_kernel,
        in_specs=[smem] + [vmem] * 10,
        out_shape=(
            shape((HEADS, 2 * HD, TOK), BF),
            shape((HEADS, 2, TOK)),
            shape((LAND, 2 * HD)),
        ),
        scratch_shapes=region[:2] + [pltpu.VMEM((LAND, 2 * HD), F32)],
        compiler_params=pltpu.CompilerParams(vmem_limit_bytes=VMEM),
        cost_estimate=pl.CostEstimate(flops=2**31, bytes_accessed=2**22, transcendentals=2**20),
    )(place, own, top, bottom, left, right, marks, *near)

    out_q, dkv = pl.pallas_call(
        window_kernel,
        in_specs=[smem] + [vmem] * 7,
        out_shape=(
            shape((HEADS, TOK, 2 * HD), BF),
            shape((6 * STRIP, 2 * HD)),
        ),
        scratch_shapes=region,
        compiler_params=pltpu.CompilerParams(vmem_limit_bytes=VMEM),
        cost_estimate=pl.CostEstimate(flops=2**32, bytes_accessed=2**22, transcendentals=2**20),
    )(place, own, top, bottom, left, right, part, stats)
    grads = call(land_sum_kernel, shape((256, 128)), nbytes=2**18, after=(out_q,))(
        swap(dmark.reshape(64, 4, 128), BLOCKS).reshape(256, 128)
    )
    grads = swap(grads.reshape(64, 4, 128), BLOCKS).reshape(256, 128)

    land, proj, sides = pl.pallas_call(
        land_grad_kernel,
        grid=(1,),
        in_specs=[
            pl.BlockSpec((HEADS, 1, TOK, 2 * HD), lambda i: (0, 0, 0, 0)),
            pl.BlockSpec((LAND, 2 * HD), lambda i: (0, 0)),
            pl.BlockSpec((512, 128), lambda i: (0, 0)),
            pl.BlockSpec((256, 128), lambda i: (0, 0)),
            pl.BlockSpec((STRIP, 2 * HD), lambda i: (0, 0)),
            pl.BlockSpec((STRIP, 2 * HD), lambda i: (5, 0)),
        ],
        out_specs=[
            pl.BlockSpec((HEADS, TOK, 2 * HD), lambda i: (0, 0, 0)),
            pl.BlockSpec((8, 128, 128), lambda i: (0, 0, 0)),
            pl.BlockSpec((2, STRIP, 2 * HD), lambda i: (0, 0, 0)),
        ],
        out_shape=(
            shape((HEADS, TOK, 2 * HD)),
            shape((8, 128, 128), BF),
            shape((2, STRIP, 2 * HD), BF),
        ),
        compiler_params=pltpu.CompilerParams(vmem_limit_bytes=VMEM),
        cost_estimate=pl.CostEstimate(flops=2**29, bytes_accessed=2**21, transcendentals=2**18),
    )(own, weight, marks, grads, dkv, dkv)
    from_right = shift(sides[0], "y", -1)
    from_left = shift(sides[1], "y", 1)
    to_above, to_below = call(edge_kernel, (shape((4, 64, 2 * HD), BF),) * 2, nbytes=2**18)(
        dkv, from_left, from_right
    )
    from_below = shift(to_above, "z", -1)
    from_above = shift(to_below, "z", 1)

    proj = swap(call(proj_sum_kernel, shape((8, 128, 128), BF), after=(to_above, to_below))(swap(proj, "z")), "y")
    final = call(final_pack_kernel, shape((HEADS, 3, TOK, 128), BF), nbytes=2**20)(
        out_q, land, dkv, from_left, from_right, from_above, from_below, proj
    )
    *tokens, grad_proj = call(
        unpack_kernel,
        (shape((TOK, feats), BF),) * 4 + (shape((HEADS, HD, LAND)),),
        nbytes=2**20,
    )(swap(final, GROUP))
    return *(a.reshape(rows, cols, feats) for a in tokens), grad_proj


def solution(mesh):
    total_rows, total_cols = mesh.devices.shape
    fine = Mesh(mesh.devices.reshape(total_rows // 2, 2, total_cols // 4, 4), ("z", "core", "y", "x"))
    tokens = P(("z", "core"), ("y", "x"), None)
    return jax.shard_map(
        per_device,
        mesh=fine,
        in_specs=(tokens, tokens, tokens, P(), tokens),
        out_specs=(tokens, tokens, tokens, tokens, P()),
        check_vma=False,
    )
```

```python
import jax
import jax.numpy as jnp
from jax import lax
from jax.experimental import pallas as pl
from jax.experimental.pallas import tpu as pltpu
from jax.sharding import Mesh, PartitionSpec as P

RAD = 8
HEADS = 8
HD = 64
LAND = 256
TOK = 128
STRIP = 384
SCALE = HD**-0.5
NEG = -1e30
VMEM = 24 * 2**20
PACK_VMEM = 2**26 - 2**18
BF = jnp.bfloat16
F32 = jnp.float32
GROUP = ("core", "x")
BLOCKS = ("z", "y")
NT = (((1,), (1,)), ((), ()))


def call(body, outs, flops=0, nbytes=0, trans=0, after=()):
    def ordered(*refs):
        return body(*refs[len(after) :])

    return lambda *args: pl.pallas_call(
        ordered,
        out_shape=outs,
        in_specs=[pl.BlockSpec(memory_space=pl.ANY)] * len(after)
        + [pl.BlockSpec(memory_space=pltpu.VMEM)] * len(args),
        compiler_params=pltpu.CompilerParams(vmem_limit_bytes=VMEM),
        cost_estimate=pl.CostEstimate(flops=flops, bytes_accessed=nbytes, transcendentals=trans),
    )(*after, *args)


def dot(a, b, dims=(((1,), (0,)), ((), ()))):
    return lax.dot_general(a, b, dims, preferred_element_type=F32)


def split_hi_lo(x):
    hi = x.astype(BF)
    return hi, (x - hi.astype(F32)).astype(BF)


def pack_kernel(k_hbm, v_hbm, q_hbm, g_hbm, out_ref, held, sems):
    copies = [
        pltpu.make_async_copy(source, held.at[i], sems.at[i])
        for i, source in enumerate((k_hbm, v_hbm, q_hbm, g_hbm))
    ]
    for copy in copies:
        copy.start()
    for part in range(2):
        copies[2 * part].wait()
        copies[2 * part + 1].wait()
        for h in range(HEADS):
            at = slice(h * HD, (h + 1) * HD)
            out_ref[h, part] = jnp.concatenate([held[2 * part, :, at], held[2 * part + 1, :, at]], 1)


def final_pack_kernel(out_q_ref, land_ref, dkv_ref, left_ref, right_ref, above_ref, below_ref, proj_ref, out_ref):
    proj = sum_of_eight(proj_ref)
    for h in range(HEADS):
        half, strip = h // 4, h % 4
        base = (strip + 1) * STRIP + 64 + half * TOK
        grads = land_ref[h] + dkv_ref[base : base + TOK]
        if strip == 0:
            grads += left_ref[64 + half * TOK : 64 + half * TOK + TOK].astype(F32)
        if strip == 3:
            grads += right_ref[64 + half * TOK : 64 + half * TOK + TOK].astype(F32)
        zero = jnp.zeros((64, 2 * HD), F32)
        if half == 0:
            grads += jnp.concatenate([above_ref[strip].astype(F32), zero], 0)
        else:
            grads += jnp.concatenate([zero, below_ref[strip].astype(F32)], 0)
        out_ref[h, 0] = out_q_ref[h]
        out_ref[h, 1] = grads.astype(BF)
        out_ref[h, 2] = proj


def edge_kernel(dkv_ref, left_ref, right_ref, top_ref, bottom_ref):
    for strip in range(4):
        base = (strip + 1) * STRIP
        for ref, first in ((top_ref, 0), (bottom_ref, 320)):
            grads = dkv_ref[base + first : base + first + 64]
            if strip == 0:
                grads += left_ref[first : first + 64].astype(F32)
            if strip == 3:
                grads += right_ref[first : first + 64].astype(F32)
            ref[strip] = grads.astype(BF)


def unpack_kernel(in_ref, att_ref, dq_ref, dk_ref, dv_ref, proj_ref):
    for i in range(HEADS // 2):
        at = slice(i * 2 * HD, (i + 1) * 2 * HD)
        for part, first_ref, second_ref in ((0, att_ref, dq_ref), (1, dk_ref, dv_ref)):
            even, odd = in_ref[2 * i, part], in_ref[2 * i + 1, part]
            first_ref[:, at] = jnp.concatenate([even[:, :HD], odd[:, :HD]], 1)
            second_ref[:, at] = jnp.concatenate([even[:, HD:], odd[:, HD:]], 1)
    for h in range(HEADS):
        proj_ref[h, :, :128] = in_ref[h, 2, :HD].astype(F32)
        proj_ref[h, :, 128:] = in_ref[h, 2, HD:].astype(F32)


def sums_kernel(kvqg_ref, w_ref, out_ref):
    kv = kvqg_ref[:, 0].reshape(HEADS * TOK, 2 * HD)
    logits = dot(w_ref[...], kv, NT)
    top = jnp.max(logits, 1, keepdims=True)
    terms = jnp.exp(logits - top)
    total = jnp.sum(terms, 1, keepdims=True)
    hi, lo = split_hi_lo(terms)
    sums = dot(hi, kv) + dot(lo, kv)
    lane = lax.broadcasted_iota(jnp.int32, (LAND, 2 * HD), 1)
    stats = jnp.where(lane < HD, top, total)
    for j in range(4):
        out_ref[pl.ds(j, 64, stride=8), :] = sums[64 * j : 64 * j + 64]
        out_ref[pl.ds(4 + j, 64, stride=8), :] = stats[64 * j : 64 * j + 64]


def means_kernel(in_ref, out_ref):
    got = in_ref[...]
    stats = pltpu.roll(got, 4, 1)
    other = pltpu.roll(stats, HD, 2)
    low = lax.broadcasted_iota(jnp.int32, got.shape, 2) < HD
    tops = jnp.where(low, stats, other)
    totals = jnp.where(low, other, stats)
    top = jnp.max(tops, 0, keepdims=True)
    factor = jnp.exp(tops - top)
    total = jnp.sum(factor * totals, 0)
    mean = jnp.sum(factor * got, 0) / total
    log_total = top[0] + jnp.log(total)
    row = lax.broadcasted_iota(jnp.int32, mean.shape, 0)
    result = jnp.where(row < 4, mean, pltpu.roll(log_total, 4, 0))
    out_ref[...] = jnp.broadcast_to(result[None], out_ref.shape)


def land_sum_kernel(in_ref, out_ref):
    grads = jnp.sum(in_ref[...].reshape(32, 8, 2 * HD), 0)
    grads = grads + pltpu.roll(grads, 4, 0)
    out_ref[...] = jnp.broadcast_to(grads[None], (32, 8, 2 * HD)).reshape(out_ref.shape)


def sum_of_eight(in_ref):
    total = in_ref[0].astype(F32)
    for i in range(1, 8):
        total += in_ref[i].astype(F32)
    return total.astype(BF)


def proj_sum_kernel(in_ref, out_ref):
    out_ref[...] = jnp.broadcast_to(sum_of_eight(in_ref)[None], out_ref.shape)


def rows_of(ref, first, stride=8):
    return jnp.concatenate([ref[pl.ds(first + j, 64, stride=stride), :] for j in range(4)], 0)


def fill_mask(mask):
    key = lax.broadcasted_iota(jnp.int32, (768, TOK), 0)
    query = lax.broadcasted_iota(jnp.int32, (768, TOK), 1)
    row_gap = ((key >> 3) & 31) - 8 - (query >> 3)
    col_gap = ((key >> 8) - 1) * 8 + (key & 7) - (query & 7)
    near = (row_gap >= -RAD) & (row_gap <= RAD) & (col_gap >= -RAD) & (col_gap <= RAD)
    mask[...] = jnp.where(near, 0.0, NEG)


def edge_bias(place_ref, strip, half):
    column = lax.broadcasted_iota(jnp.int32, (768, 1), 0)
    key_row, key_slab = (column >> 3) & 31, column >> 8
    low_row = jnp.where((place_ref[0] == 0) & (half == 0), 8, 0)
    high_row = jnp.where((place_ref[0] == place_ref[2] - 1) & (half == 1), 24, 32)
    low_slab = jnp.where((place_ref[1] == 0) & (strip == 0), 1, 0)
    high_slab = jnp.where((place_ref[1] == place_ref[3] - 1) & (strip == 3), 1, 2)
    inside = (key_row >= low_row) & (key_row < high_row) & (key_slab >= low_slab) & (key_slab <= high_slab)
    return jnp.where(inside, 0.0, NEG)


def query_pair(query_grad):
    lane = lax.broadcasted_iota(jnp.int32, (TOK, 2 * HD), 1)
    wide = query_grad.astype(F32)
    upper = jnp.where(lane < HD, wide * SCALE, 0.0).astype(BF)
    lower = jnp.where(lane < HD, 0.0, wide).astype(BF)
    return wide, jnp.concatenate([upper, lower], 0)


def slab_starts(strip, half):
    return [pl.multiple_of((strip + j) * STRIP + half * TOK, 128) for j in range(3)]


def fill_strip(kvqg_ref, top_ref, bottom_ref, ext, x, base):
    ext[base : base + 64] = top_ref[x]
    ext[base + 64 : base + 192] = kvqg_ref[x, 0]
    ext[base + 192 : base + 320] = kvqg_ref[4 + x, 0]
    ext[base + 320 : base + 384] = bottom_ref[x]


def fill_region(kvqg_ref, top_ref, bottom_ref, left_ref, right_ref, ext):
    for x in range(4):
        fill_strip(kvqg_ref, top_ref, bottom_ref, ext, x, (x + 1) * STRIP)
    ext[0:STRIP] = left_ref[...]
    ext[5 * STRIP : 6 * STRIP] = right_ref[...]


def near_kernel(place_ref, kvqg_ref, top_ref, bottom_ref, near_ref, stat_ref, ext_t, mask, ext):
    for x in range(4):
        fill_strip(kvqg_ref, top_ref, bottom_ref, ext, x, x * STRIP)
    for i in range(12):
        ext_t[:, i * 128 : (i + 1) * 128] = ext[i * 128 : (i + 1) * 128].T
    fill_mask(mask)

    def tile(step, carry):
        strip, half = 1 + (step & 1), step >> 1
        starts = slab_starts(strip - 1, half)
        _, pair = query_pair(kvqg_ref[half * 4 + strip, 1])
        keys = jnp.concatenate([ext[pl.ds(s, 256), :] for s in starts], 0)
        score = dot(keys, pair[:TOK], NT) + (mask[...] + edge_bias(place_ref, strip, half))
        top = jnp.max(score, 0, keepdims=True)
        terms = jnp.exp(score - top)
        stat_ref[step] = jnp.concatenate([top, jnp.sum(terms, 0, keepdims=True)], 0)
        slabs_t = jnp.concatenate([ext_t[HD:, pl.ds(s, 256)] for s in starts], 1)
        near_ref[step] = dot(slabs_t, terms.astype(BF))
        return carry

    lax.fori_loop(0, 4, tile, 0, unroll=2)


def forward_kernel(
    place_ref, kvqg_ref, top_ref, bottom_ref, left_ref, right_ref, marks_ref,
    near_ref, near_stat_ref, own_t_ref, mask,
    part_ref, stat_ref, dmark_ref,
    ext, ext_t, dmark,
):
    fill_region(kvqg_ref, top_ref, bottom_ref, left_ref, right_ref, ext)
    ext_t[:, STRIP : 5 * STRIP] = own_t_ref[...]
    for i in (0, 1, 2, 15, 16, 17):
        ext_t[:, i * 128 : (i + 1) * 128] = ext[i * 128 : (i + 1) * 128].T
    kv_mark = rows_of(marks_ref, 0).astype(BF)
    kv_mark_t = jnp.concatenate([kv_mark[0:128].T, kv_mark[128:256].T], 1)
    dmark[...] = jnp.zeros_like(dmark)

    def whole_tile(step, carry):
        strip, half = 3 * (step & 1), step >> 1
        index = half * 4 + strip
        starts = slab_starts(strip, half)
        wide, pair = query_pair(kvqg_ref[index, 1])
        near_keys = jnp.concatenate([ext[pl.ds(s, 256), :] for s in starts], 0)
        near_score = dot(near_keys, pair[:TOK], NT) + (mask[...] + edge_bias(place_ref, strip, half))
        both = dot(kv_mark, pair, NT)
        mark_score, mark_inner = both[:, :TOK], both[:, TOK:]
        top = jnp.maximum(
            jnp.max(near_score, 0, keepdims=True), jnp.max(mark_score, 0, keepdims=True)
        )
        near_terms, mark_terms = jnp.exp(near_score - top), jnp.exp(mark_score - top)
        total = jnp.sum(near_terms, 0, keepdims=True) + jnp.sum(mark_terms, 0, keepdims=True)
        share = 1.0 / total
        prob = mark_terms * share
        weights = prob.astype(BF)
        near_weights = (near_terms * share).astype(BF)
        slabs_t = jnp.concatenate([ext_t[HD:, pl.ds(s, 256)] for s in starts] + [kv_mark_t[HD:]], 1)
        mixed = dot(slabs_t, jnp.concatenate([near_weights, weights], 0))
        delta = jnp.sum(wide.T[HD:] * mixed, 0, keepdims=True)
        dscore = (prob * (mark_inner - delta)).astype(BF)
        part_ref[index] = jnp.concatenate([mixed, dot(kv_mark_t[:HD], dscore)], 0).astype(BF)
        stat_ref[index] = jnp.concatenate([top + jnp.log(total), delta], 0)
        dmark[...] += dot(jnp.concatenate([dscore, weights], 1), pair)
        return carry

    def mark_tile(step, carry):
        index = (step >> 1) * 4 + 1 + (step & 1)
        wide, pair = query_pair(kvqg_ref[index, 1])
        both = dot(kv_mark, pair, NT)
        score, inner = both[:, :TOK], both[:, TOK:]
        near_top, near_total = near_stat_ref[step, 0:1], near_stat_ref[step, 1:2]
        top = jnp.maximum(near_top, jnp.max(score, 0, keepdims=True))
        terms = jnp.exp(score - top)
        near_factor = jnp.exp(near_top - top)
        total = near_factor * near_total + jnp.sum(terms, 0, keepdims=True)
        share = 1.0 / total
        prob = terms * share
        weights = prob.astype(BF)
        mixed = dot(kv_mark_t[HD:], weights) + near_ref[step] * (near_factor * share)
        delta = jnp.sum(wide.T[HD:] * mixed, 0, keepdims=True)
        dscore = (prob * (inner - delta)).astype(BF)
        part_ref[index] = jnp.concatenate([mixed, dot(kv_mark_t[:HD], dscore)], 0).astype(BF)
        stat_ref[index] = jnp.concatenate([top + jnp.log(total), delta], 0)
        dmark[...] += dot(jnp.concatenate([dscore, weights], 1), pair)
        return carry

    lax.fori_loop(0, 4, whole_tile, 0, unroll=4)
    lax.fori_loop(0, 4, mark_tile, 0, unroll=4)
    for j in range(4):
        dmark_ref[pl.ds(j, 64, stride=4), :] = dmark[64 * j : 64 * j + 64]


def window_kernel(
    place_ref, kvqg_ref, top_ref, bottom_ref, left_ref, right_ref, part_ref, stat_ref,
    out_ref, dkv_ref,
    ext, ext_t, mask,
):
    fill_region(kvqg_ref, top_ref, bottom_ref, left_ref, right_ref, ext)
    for i in range(18):
        ext_t[:, i * 128 : (i + 1) * 128] = ext[i * 128 : (i + 1) * 128].T
    fill_mask(mask)
    dkv_ref[...] = jnp.zeros_like(dkv_ref)

    def tile(index, carry):
        strip, half = index & 3, index >> 2
        starts = slab_starts(strip, half)
        _, pair = query_pair(kvqg_ref[index, 1])
        stats = stat_ref[index]
        both = dot(jnp.concatenate([ext[pl.ds(s, 256), :] for s in starts], 0), pair, NT)
        score = both[:, :TOK] + (mask[...] + edge_bias(place_ref, strip, half))
        prob = jnp.exp(score - stats[0:1])
        dscore = (prob * (both[:, TOK:] - stats[1:2])).astype(BF)
        slabs_t = jnp.concatenate([ext_t[:HD, pl.ds(s, 256)] for s in starts], 1)
        part = part_ref[index].astype(F32)
        dquery = (dot(slabs_t, dscore) + part[HD:]) * SCALE
        out_ref[index] = jnp.concatenate([part[:HD], dquery], 0).T.astype(BF)
        dkv = dot(jnp.concatenate([dscore, prob.astype(BF)], 1), pair)
        for j, s in enumerate(starts):
            dkv_ref[pl.ds(s, 256), :] += dkv[256 * j : 256 * j + 256]
        return carry

    lax.fori_loop(0, 8, tile, 0, unroll=2)


def land_grad_kernel(kvqg_ref, w_ref, marks_ref, grads_ref, first_ref, last_ref, out_ref, proj_ref, side_ref):
    side_ref[0] = first_ref[...].astype(BF)
    side_ref[1] = last_ref[...].astype(BF)
    kv = kvqg_ref[:, 0].reshape(HEADS * TOK, 2 * HD)
    weight = w_ref[...]
    log_total = rows_of(marks_ref, 4)[:, :1]
    grads = rows_of(grads_ref, 0, 4)
    column = jnp.sum(rows_of(marks_ref, 0) * grads, 1, keepdims=True)
    prob = jnp.exp(dot(weight, kv, NT) - log_total)
    hi, lo = split_hi_lo(grads)
    dprob = dot(hi, kv, NT) + dot(lo, kv, NT)
    dlogit = prob * (dprob - column)
    dlogit_bf, dlogit_lo = split_hi_lo(dlogit)
    prob_bf, prob_lo = split_hi_lo(prob)
    flip = lambda a: jnp.concatenate([a[:128].T, a[128:].T], 1)
    hi_t, lo_t, weight_t = flip(hi), flip(lo), flip(weight)
    left_t = jnp.concatenate([hi_t, weight_t, hi_t, weight_t, lo_t], 1)
    right = jnp.concatenate([prob_bf, dlogit_bf, prob_lo, dlogit_lo, prob_bf], 0)
    land = dot(left_t, right)
    for i in range(HEADS):
        out_ref[i] = land[:, i * TOK : (i + 1) * TOK].T
    proj = dot(dlogit_bf, kv) + dot(dlogit_lo, kv)
    proj = jnp.concatenate([proj[128 * i : 128 * i + 128].T[:HD] for i in range(2)], 0)
    proj_ref[...] = jnp.broadcast_to(proj.astype(BF)[None], proj_ref.shape)


def shape(dims, dtype=F32):
    return jax.ShapeDtypeStruct(dims, dtype)


def swap(x, axes):
    return lax.all_to_all(x, axes, 0, 0, tiled=True)


def shift(x, axis, step):
    n = lax.axis_size(axis)
    return lax.ppermute(x, axis, [(i, i + step) for i in range(n) if 0 <= i + step < n])


def per_device(query_feats, key_feats, value_feats, proj_weight, cotangent):
    rows, cols, feats = query_feats.shape
    flat = lambda a: a.reshape(TOK, feats)
    head = lax.axis_index("core") * lax.axis_size("x") + lax.axis_index("x")
    weight = lax.dynamic_index_in_dim(proj_weight, head, 0, keepdims=False)
    weight = jnp.pad(weight.T, ((0, 0), (0, HD)))
    place = jnp.stack(
        [lax.axis_index("z"), lax.axis_index("y"), lax.axis_size("z"), lax.axis_size("y")]
    ).astype(jnp.int32)

    packed = pl.pallas_call(
        pack_kernel,
        in_specs=[pl.BlockSpec(memory_space=pltpu.HBM)] * 4,
        out_shape=shape((HEADS, 2, TOK, 2 * HD), BF),
        scratch_shapes=[pltpu.VMEM((4, TOK, feats), BF), pltpu.SemaphoreType.DMA((4,))],
        compiler_params=pltpu.CompilerParams(vmem_limit_bytes=PACK_VMEM),
        cost_estimate=pl.CostEstimate(flops=0, bytes_accessed=2**20, transcendentals=0),
    )(flat(key_feats), flat(value_feats), flat(query_feats), flat(cotangent))
    own = swap(packed, GROUP)

    sums = call(sums_kernel, shape((512, 128)), flops=2 * 3 * 2**25, nbytes=2**19, trans=2**18)(own, weight)

    top = shift(own[4:8, 0, 64:], "z", 1)
    bottom = shift(own[0:4, 0, :64], "z", -1)
    strip_of = lambda x: jnp.concatenate([top[x], own[x, 0], own[4 + x, 0], bottom[x]], 0)
    left = shift(strip_of(3), "y", 1)
    right = shift(strip_of(0), "y", -1)

    means = call(means_kernel, shape((64, 8, 128)), nbytes=2**19)(swap(sums.reshape(64, 8, 128), BLOCKS))
    marks = swap(means, BLOCKS).reshape(512, 128)

    smem, vmem = pl.BlockSpec(memory_space=pltpu.SMEM), pl.BlockSpec(memory_space=pltpu.VMEM)
    region = [
        pltpu.VMEM((6 * STRIP, 2 * HD), BF),
        pltpu.VMEM((2 * HD, 6 * STRIP), BF),
        pltpu.VMEM((768, TOK), F32),
    ]
    near = pl.pallas_call(
        near_kernel,
        in_specs=[smem] + [vmem] * 3,
        out_shape=(
            shape((4, HD, TOK)),
            shape((4, 2, TOK)),
            shape((2 * HD, 4 * STRIP), BF),
            shape((768, TOK)),
        ),
        scratch_shapes=[pltpu.VMEM((4 * STRIP, 2 * HD), BF)],
        compiler_params=pltpu.CompilerParams(vmem_limit_bytes=VMEM),
        cost_estimate=pl.CostEstimate(flops=2**31, bytes_accessed=2**22, transcendentals=2**20),
    )(place, own, top, bottom)
    part, stats, dmark = pl.pallas_call(
        forward_kernel,
        in_specs=[smem] + [vmem] * 10,
        out_shape=(
            shape((HEADS, 2 * HD, TOK), BF),
            shape((HEADS, 2, TOK)),
            shape((LAND, 2 * HD)),
        ),
        scratch_shapes=region[:2] + [pltpu.VMEM((LAND, 2 * HD), F32)],
        compiler_params=pltpu.CompilerParams(vmem_limit_bytes=VMEM),
        cost_estimate=pl.CostEstimate(flops=2**31, bytes_accessed=2**22, transcendentals=2**20),
    )(place, own, top, bottom, left, right, marks, *near)

    out_q, dkv = pl.pallas_call(
        window_kernel,
        in_specs=[smem] + [vmem] * 7,
        out_shape=(
            shape((HEADS, TOK, 2 * HD), BF),
            shape((6 * STRIP, 2 * HD)),
        ),
        scratch_shapes=region,
        compiler_params=pltpu.CompilerParams(vmem_limit_bytes=VMEM),
        cost_estimate=pl.CostEstimate(flops=2**32, bytes_accessed=2**22, transcendentals=2**20),
    )(place, own, top, bottom, left, right, part, stats)
    grads = call(land_sum_kernel, shape((256, 128)), nbytes=2**18, after=(out_q,))(
        swap(dmark.reshape(64, 4, 128), BLOCKS).reshape(256, 128)
    )
    grads = swap(grads.reshape(64, 4, 128), BLOCKS).reshape(256, 128)

    land, proj, sides = pl.pallas_call(
        land_grad_kernel,
        grid=(1,),
        in_specs=[
            pl.BlockSpec((HEADS, 1, TOK, 2 * HD), lambda i: (0, 0, 0, 0)),
            pl.BlockSpec((LAND, 2 * HD), lambda i: (0, 0)),
            pl.BlockSpec((512, 128), lambda i: (0, 0)),
            pl.BlockSpec((256, 128), lambda i: (0, 0)),
            pl.BlockSpec((STRIP, 2 * HD), lambda i: (0, 0)),
            pl.BlockSpec((STRIP, 2 * HD), lambda i: (5, 0)),
        ],
        out_specs=[
            pl.BlockSpec((HEADS, TOK, 2 * HD), lambda i: (0, 0, 0)),
            pl.BlockSpec((8, 128, 128), lambda i: (0, 0, 0)),
            pl.BlockSpec((2, STRIP, 2 * HD), lambda i: (0, 0, 0)),
        ],
        out_shape=(
            shape((HEADS, TOK, 2 * HD)),
            shape((8, 128, 128), BF),
            shape((2, STRIP, 2 * HD), BF),
        ),
        compiler_params=pltpu.CompilerParams(vmem_limit_bytes=VMEM),
        cost_estimate=pl.CostEstimate(flops=2**29, bytes_accessed=2**21, transcendentals=2**18),
    )(own, weight, marks, grads, dkv, dkv)
    from_right = shift(sides[0], "y", -1)
    from_left = shift(sides[1], "y", 1)
    to_above, to_below = call(edge_kernel, (shape((4, 64, 2 * HD), BF),) * 2, nbytes=2**18)(
        dkv, from_left, from_right
    )
    from_below = shift(to_above, "z", -1)
    from_above = shift(to_below, "z", 1)

    proj = swap(call(proj_sum_kernel, shape((8, 128, 128), BF), after=(to_above, to_below))(swap(proj, "z")), "y")
    final = call(final_pack_kernel, shape((HEADS, 3, TOK, 128), BF), nbytes=2**20)(
        out_q, land, dkv, from_left, from_right, from_above, from_below, proj
    )
    *tokens, grad_proj = call(
        unpack_kernel,
        (shape((TOK, feats), BF),) * 4 + (shape((HEADS, HD, LAND)),),
        nbytes=2**20,
    )(swap(final, GROUP))
    return *(a.reshape(rows, cols, feats) for a in tokens), grad_proj


def solution(mesh):
    total_rows, total_cols = mesh.devices.shape
    fine = Mesh(mesh.devices.reshape(total_rows // 2, 2, total_cols // 4, 4), ("z", "core", "y", "x"))
    tokens = P(("z", "core"), ("y", "x"), None)
    return jax.shard_map(
        per_device,
        mesh=fine,
        in_specs=(tokens, tokens, tokens, P(), tokens),
        out_specs=(tokens, tokens, tokens, tokens, P()),
        check_vma=False,
    )
```
